128 devices in a mesh: area: 8 (over y, core), depth: 16 (over x, z).
Axes of the slice: x: 4, y: 4, z: 4, core: 2. Of those that a mesh axis runs over, the one named last changes fastest.
Arguments:
- field: float32 [512, 512, 512], P('depth', 'area'), may hold values from -6 to 6
- materials: int32 [512, 512, 512], P('depth', 'area'), may hold values from 0 to 15
- tf_table: float32 [4, 16], replicated, may hold values from 0 to 1, as said below
- view_order: int32 [2, 16], replicated, may hold values from 0 to 15, each once within a row
- shear_offset: int32 [16], replicated, may hold values from 0 to 63, as said below
Outputs:
- image: float32 [2, 4, 512, 512], P(None, None, ('area', 'depth'))
The draws below stay inside these ranges and needn't reach their ends.
Inputs may be any that keep to these rules, and one draw needn't show every extreme that they name: `shear_offset`: every entry lies in 0 to 63; some layer has offset 0 and some layer has offset 64 - 1. `view_order`: each row is a permutation of the depth layers. `tf_table`: the colour rows lie in 0.05 to 0.6; the opacity row lies in 0.02 / 32 to 0.5 / 32.
All inputs are finite; a program needn't handle non-finite values.
Results may differ from the reference program's by a relative error of at most 0.0003.
Values sent between devices are 32-bit elements; how exact they have to be, the bound alone decides.
A program may use at most 128 MiB of HBM per device.

```python
import jax
import jax.numpy as jnp
from jax import lax

BZ = 32
BY = 64
BX = 512
TFN = 16
NZ = 512
NY = 512
N_DEPTH = 16


def draw_shear_offset(key, part):
    first_key = jax.random.fold_in(key, 11)
    second_key = jax.random.fold_in(key, 12)
    values = jax.random.randint(first_key, (N_DEPTH,), 0, BY, dtype=jnp.int32)
    places = jax.random.permutation(second_key, N_DEPTH)
    values = values.at[places[0]].set(BY - 1)
    values = values.at[places[1]].set(0)
    return values.astype(jnp.int32)


def draw_tf_table(key, part):
    colour_key = jax.random.fold_in(key, 21)
    opacity_key = jax.random.fold_in(key, 22)
    colours = jax.random.uniform(colour_key, (3, TFN), jnp.float32, 0.05, 0.6)
    opacities = jax.random.uniform(opacity_key, (1, TFN), jnp.float32, 0.02, 0.5) / jnp.float32(BZ)
    return jnp.concatenate([colours, opacities], axis=0).astype(jnp.float32)


def set_ends(values, rng, smallest, top_value):
    longest = values.shape.index(max(values.shape))
    spots = []
    for shift in (0, 1):
        where = [jax.random.randint(jax.random.fold_in(rng, axis), (), 0, length) for axis, length in enumerate(values.shape)]
        where[longest] = (where[longest] + shift) % values.shape[longest]
        spots.append(tuple(where))
    return values.at[spots[0]].set(smallest).at[spots[1]].set(top_value)


def steps_of(rng, dims, split, smallest, top_value):
    gain = 1.0
    for axis_at, shards_of in split:
        draws = jax.random.uniform(jax.random.fold_in(jax.random.fold_in(rng, 6), axis_at), (shards_of,), jnp.float32, smallest / len(split), top_value / len(split))
        gain = gain * jnp.repeat(jnp.exp(draws), dims[axis_at] // shards_of).reshape((-1,) + (1,) * (len(dims) - 1 - axis_at))
    return gain


def scatter_about(stream_key, shape, scale, most, cuts=(), kind=jnp.bfloat16):
    entries = scale * jax.random.normal(stream_key, shape, jnp.float32)
    if cuts:
        entries = entries * steps_of(stream_key, shape, cuts, -0.22, 0.18)
    return jnp.clip(entries, -most, most).astype(kind)


def setup_inputs(seed: int = 0) -> dict:
    arg_keys = jax.random.split(jax.random.key(seed), 6)
    return {
        "field": scatter_about(arg_keys[0], (NZ, NY, BX), 1.0, 6.0, ((0, 16), (1, 8)), jnp.float32),
        "materials": set_ends(jax.random.randint(arg_keys[1], (NZ, NY, BX), 0, TFN), jax.random.fold_in(arg_keys[1], 1), 0, TFN - 1).astype(jnp.int32),
        "tf_table": draw_tf_table(jax.random.fold_in(arg_keys[5], 71), 0),
        "view_order": jax.vmap(lambda own: jax.random.permutation(own, N_DEPTH))(jax.random.split(arg_keys[3], 2)).reshape((2, N_DEPTH)).astype(jnp.int32),
        "shear_offset": draw_shear_offset(jax.random.fold_in(arg_keys[5], 71), 0),
    }


def classify(padded, materials, tf_table):
    widened = jnp.pad(padded, ((0, 0), (0, 0), (1, 1)))
    center = widened[1:-1, 1:-1, 1:-1]
    grad_z = 0.5 * (widened[2:, 1:-1, 1:-1] - widened[:-2, 1:-1, 1:-1])
    grad_y = 0.5 * (widened[1:-1, 2:, 1:-1] - widened[1:-1, :-2, 1:-1])
    grad_x = 0.5 * (widened[1:-1, 1:-1, 2:] - widened[1:-1, 1:-1, :-2])
    grad_sq = grad_z * grad_z + grad_y * grad_y + grad_x * grad_x
    shade = 0.3 + 0.7 * jnp.abs(0.48 * grad_z + 0.6 * grad_y + 0.64 * grad_x) / jnp.sqrt(grad_sq + 1.0)
    looked = []
    for channel in range(4):
        total = jnp.zeros(materials.shape, jnp.float32)
        for entry in range(tf_table.shape[1]):
            total = total + jnp.where(materials == entry, tf_table[channel, entry], jnp.float32(0.0))
        looked.append(total)
    opacity_cell = looked[3] * (1.0 - jnp.exp(-0.25 * (center * center + grad_sq)))
    colour_cell = jnp.stack(looked[:3]) * (shade * opacity_cell)[None]
    return (colour_cell, opacity_cell)

def march(colour_cell, opacity_cell):
    log_keep = jnp.log1p(-opacity_cell)
    before = jnp.exp(jnp.cumsum(log_keep, axis=0) - log_keep)
    colour = lax.optimization_barrier(jnp.sum(colour_cell * before[None], axis=1))
    opacity = 1.0 - jnp.exp(lax.optimization_barrier(jnp.sum(log_keep, axis=0)))
    return jnp.concatenate([colour, opacity[None]], axis=0)

def composite(stack, view_order):
    results = []
    for view_idx in range(2):
        sequence = jnp.take(stack[:, view_idx], view_order[view_idx], axis=0)

        def over_step(state_pair, layer_img):
            colour, opacity = state_pair
            colour = colour + (1.0 - opacity)[None] * layer_img[:3]
            opacity = opacity + (1.0 - opacity) * layer_img[3]
            return ((colour, opacity), None)
        start = (jnp.zeros((3,) + sequence.shape[2:], jnp.float32), jnp.zeros(sequence.shape[2:], jnp.float32))
        (colour, opacity), unused = lax.scan(over_step, start, sequence)
        results.append(jnp.concatenate([colour, opacity[None]], axis=0))
    return jnp.stack(results)

def reference(field, materials, tf_table, view_order, shear_offset):
    padded_all = jnp.pad(field, ((1, 1), (1, 1), (0, 0)))
    rows_all = field.shape[1]

    def one_layer(layer_idx):
        layer_idx = layer_idx.astype(jnp.int32)
        start = (layer_idx * BZ).astype(jnp.int32)
        zero = jnp.int32(0)
        block = lax.dynamic_slice(padded_all, (start, zero, zero), (BZ + 2, rows_all + 2, BX))
        mats = lax.dynamic_slice(materials, (start, zero, zero), (BZ, rows_all, BX))
        colour_cell, opacity_cell = classify(block, mats, tf_table)
        first = march(colour_cell, opacity_cell)
        second = march(colour_cell[:, ::-1], opacity_cell[::-1])
        spread = jnp.zeros((4, rows_all + BY, BX), jnp.float32)
        spread = lax.dynamic_update_slice(spread, second, (zero, shear_offset[layer_idx].astype(jnp.int32), zero))
        return jnp.stack([first, spread[:, :rows_all]])
    stack = lax.map(one_layer, jnp.arange(N_DEPTH, dtype=jnp.int32))
    return composite(stack, view_order)
```

```python
import functools

import jax
import jax.numpy as jnp
from jax import lax
from jax.experimental import pallas as pl
from jax.experimental.pallas import tpu as pltpu
from jax.sharding import PartitionSpec as P

MESH = pl.DeviceIdType.MESH
LANES = 128
SUB = 8
EXP_SCALE = -0.25 * 1.4426950408889634


def sublane_gather(table, index):
    dims = lax.GatherDimensionNumbers(
        offset_dims=(),
        collapsed_slice_dims=(0,),
        start_index_map=(0,),
        operand_batching_dims=(1,),
        start_indices_batching_dims=(1,),
    )
    return lax.gather(
        table, index[..., None], dims, (1, 1), mode=lax.GatherScatterMode.PROMISE_IN_BOUNDS
    )


def kernel(
    n_area,
    n_depth,
    field_hbm,
    mat_hbm,
    tf_hbm,
    order_hbm,
    shear_hbm,
    out_ref,
    F,
    M,
    tf_s,
    order_s,
    shear_s,
    edge_out,
    edge_in,
    state,
    own,
    near,
    window,
    send,
    recv,
    load_sem,
    small_sem,
    halo_send,
    halo_recv,
    shear_send,
    shear_recv,
    a2a_send,
    a2a_recv,
):
    planes, rows, columns = field_hbm.shape
    blocks = columns // LANES
    tiles = rows // SUB
    part = rows // n_depth
    area, depth = lax.axis_index("area"), lax.axis_index("depth")
    zero = jnp.zeros((SUB, LANES), jnp.float32)

    for b in range(blocks):
        pltpu.make_async_copy(
            field_hbm.at[:, :, pl.ds(b * LANES, LANES)],
            F.at[b + 1, pl.ds(1, planes), pl.ds(SUB, rows)],
            load_sem.at[b],
        ).start()
    for b in range(blocks):
        pltpu.make_async_copy(
            mat_hbm.at[:, :, pl.ds(b * LANES, LANES)], M.at[b], load_sem.at[blocks + b]
        ).start()
    small = [
        pltpu.make_async_copy(src, dst, small_sem.at[i])
        for i, (src, dst) in enumerate(
            ((tf_hbm, tf_s), (order_hbm, order_s), (shear_hbm, shear_s))
        )
    ]
    for copy in small:
        copy.start()

    def wait_field(b):
        pltpu.make_async_copy(
            F.at[b + 1, pl.ds(1, planes), pl.ds(SUB, rows)],
            F.at[b + 1, pl.ds(1, planes), pl.ds(SUB, rows)],
            load_sem.at[b],
        ).wait()

    def wait_mat(b):
        pltpu.make_async_copy(M.at[b], M.at[b], load_sem.at[blocks + b]).wait()

    barrier = pltpu.get_barrier_semaphore()

    def greet(i, _):
        peer = lax.rem(depth + i, n_depth)
        pl.semaphore_signal(barrier, inc=1, device_id={"depth": peer}, device_id_type=MESH)
        return 0

    lax.fori_loop(1, n_depth, greet, 0)

    @pl.when(area > 0)
    def _():
        pl.semaphore_signal(barrier, inc=1, device_id={"area": area - 1}, device_id_type=MESH)

    @pl.when(area < n_area - 1)
    def _():
        pl.semaphore_signal(barrier, inc=1, device_id={"area": area + 1}, device_id_type=MESH)

    def clear(k, _):
        for r in range(tiles + 2):
            F[0, k, pl.ds(r * SUB, SUB), :] = zero
            F[blocks + 1, k, pl.ds(r * SUB, SUB), :] = zero
        return 0

    lax.fori_loop(0, planes + 2, clear, 0)

    def clear_plane(at):
        for b in range(blocks):
            for r in range(tiles):
                F[b + 1, at, pl.ds(SUB + r * SUB, SUB), :] = zero

    @pl.when(depth == 0)
    def _():
        clear_plane(0)

    @pl.when(depth == n_depth - 1)
    def _():
        clear_plane(planes + 1)

    @pl.when(jnp.logical_and(area > 0, area < n_area - 1))
    def _():
        pl.semaphore_wait(barrier, n_depth - 1 + 2)

    @pl.when(jnp.logical_or(area == 0, area == n_area - 1))
    def _():
        pl.semaphore_wait(barrier, n_depth - 1 + 1)

    def plane_copy(b, src, dst, slot, peer):
        return pltpu.make_async_remote_copy(
            src_ref=field_hbm.at[src, :, pl.ds(b * LANES, LANES)],
            dst_ref=F.at[b + 1, dst, pl.ds(SUB, rows)],
            send_sem=halo_send.at[slot],
            recv_sem=halo_recv.at[slot],
            device_id={"depth": peer},
            device_id_type=MESH,
        )

    @pl.when(depth < n_depth - 1)
    def _():
        for b in range(blocks):
            plane_copy(b, planes - 1, 0, 0, depth + 1).start()

    @pl.when(depth > 0)
    def _():
        for b in range(blocks):
            plane_copy(b, 0, planes + 1, 1, depth - 1).start()

    for b in range(blocks):
        wait_field(b)
        for k in range(planes):
            edge_out[0, b, pl.ds(k, 1), :] = F[b + 1, k + 1, pl.ds(SUB, 1), :]
            edge_out[1, b, pl.ds(k, 1), :] = F[b + 1, k + 1, pl.ds(SUB + rows - 1, 1), :]

    def edge_copy(src, peer):
        return pltpu.make_async_remote_copy(
            src_ref=edge_out.at[src],
            dst_ref=edge_in.at[1 - src],
            send_sem=halo_send.at[2 + src],
            recv_sem=halo_recv.at[2 + src],
            device_id={"area": peer},
            device_id_type=MESH,
        )

    @pl.when(area < n_area - 1)
    def _():
        edge_copy(1, area + 1).start()

    @pl.when(area > 0)
    def _():
        edge_copy(0, area - 1).start()

    for copy in small:
        copy.wait()
    sub_id = lax.broadcasted_iota(jnp.int32, (SUB, LANES), 0)
    lane_id = lax.broadcasted_iota(jnp.int32, (SUB, LANES), 1)
    is_first, is_last = lane_id == 0, lane_id == LANES - 1
    table = []
    for channel in range(4):
        halves = []
        for half in range(2):
            values = jnp.full((SUB, LANES), tf_s[channel, half * SUB], jnp.float32)
            for entry in range(1, SUB):
                values = jnp.where(sub_id == entry, tf_s[channel, half * SUB + entry], values)
            halves.append(values)
        table.append(halves)

    def cells(b, k, row):
        mid = pl.ds(pl.multiple_of(row + SUB, SUB), SUB)
        c = F[b + 1, k + 1, mid, :]
        gz = F[b + 1, k + 2, mid, :] - F[b + 1, k, mid, :]
        gy = F[b + 1, k + 1, pl.ds(row + SUB + 1, SUB), :] - F[b + 1, k + 1, pl.ds(row + SUB - 1, SUB), :]
        before = pltpu.roll(jnp.where(is_last, F[b, k + 1, mid, :], c), 1, 1)
        after = pltpu.roll(jnp.where(is_first, F[b + 2, k + 1, mid, :], c), LANES - 1, 1)
        gx = after - before
        gm2 = 0.25 * (gz * gz + gy * gy + gx * gx)
        lit = jnp.abs(0.168 * gz + 0.21 * gy + 0.224 * gx)
        shade = 0.3 + lit * lax.rsqrt(gm2 + 1.0)
        m = M[b, k, pl.ds(pl.multiple_of(row, SUB), SUB), :]
        upper, index = m > SUB - 1, m & (SUB - 1)
        looked = [
            jnp.where(upper, sublane_gather(hi, index), sublane_gather(lo, index))
            for lo, hi in table
        ]
        a = looked[3] * (1.0 - jnp.exp2(EXP_SCALE * (c * c + gm2)))
        return looked[:3], shade * a, 1.0 - a

    def interior(b, tile):
        row = tile * SUB
        through = zero + 1.0
        front, back = [zero] * 3, [zero] * 3
        for k in range(1, planes - 1):
            colour, sa, keep = cells(b, k, row)
            weight = through * sa
            front = [f + t * weight for f, t in zip(front, colour)]
            back = [f * keep + t * sa for f, t in zip(back, colour)]
            through = through * keep
        for i, value in enumerate([through, *front, *back]):
            state[b, i, pl.ds(pl.multiple_of(row, SUB), SUB), :] = value

    def ends(b, tile):
        row = tile * SUB
        at = pl.ds(pl.multiple_of(row, SUB), SUB)
        colour0, sa0, keep0 = cells(b, 0, row)
        colour1, sa1, keep1 = cells(b, planes - 1, row)
        through = state[b, 0, at, :]
        opacity = 1.0 - through * keep0 * keep1
        for i in range(4):
            if i == 3:
                first, second = opacity, opacity
            else:
                c0, c1 = colour0[i] * sa0, colour1[i] * sa1
                first = c0 + keep0 * (state[b, 1 + i, at, :] + through * c1)
                second = c1 + keep1 * (state[b, 4 + i, at, :] + through * c0)
            own[b, i, at, :] = second
            for half in range(SUB // part):
                send[0, b, tile * (SUB // part) + half, pl.ds(i * part, part), :] = first[
                    half * part : (half + 1) * part
                ]

    def send_view(view, b):
        def one(i, _):
            peer = lax.rem(depth + i, n_depth)
            pltpu.make_async_remote_copy(
                src_ref=send.at[view, b, peer],
                dst_ref=recv.at[view, b, depth],
                send_sem=a2a_send.at[view],
                recv_sem=a2a_recv.at[view],
                device_id={"depth": peer},
                device_id_type=MESH,
            ).start()
            return 0

        lax.fori_loop(1, n_depth, one, 0)
        recv[view, b, depth] = send[view, b, depth]

    def shear_copy(b):
        return pltpu.make_async_remote_copy(
            src_ref=own.at[b],
            dst_ref=near.at[b],
            send_sem=shear_send.at[b],
            recv_sem=shear_recv.at[b],
            device_id={"area": area + 1},
            device_id_type=MESH,
        )

    offset = shear_s[depth]

    def shear(b):
        @pl.when(area > 0)
        def _():
            pltpu.make_async_copy(near.at[b], near.at[b], shear_recv.at[b]).wait()
            for i in range(4):
                window[i, pl.ds(0, rows), :] = near[b, i]

        for i in range(4):
            window[i, pl.ds(rows, rows), :] = own[b, i]
        for tile in range(tiles):
            for i in range(4):
                moved = window[i, pl.ds(rows + tile * SUB - offset, SUB), :]
                for half in range(SUB // part):
                    send[1, b, tile * (SUB // part) + half, pl.ds(i * part, part), :] = moved[
                        half * part : (half + 1) * part
                    ]
        send_view(1, b)

    @pl.when(area == 0)
    def _():
        for i in range(4):
            for tile in range(tiles):
                window[i, pl.ds(tile * SUB, SUB), :] = zero

    inner = tiles - 2
    early = 2

    def first_pass(i, _):
        b = i // inner
        tile = 1 + i % inner

        @pl.when(tile == 1)
        def _():
            wait_mat(b)

        interior(b, tile)
        return 0

    lax.fori_loop(0, early * inner, first_pass, 0)

    @pl.when(depth > 0)
    def _():
        at = F.at[pl.ds(1, blocks), 0, pl.ds(SUB, rows)]
        pltpu.make_async_copy(at, at, halo_recv.at[0]).wait()

    @pl.when(depth < n_depth - 1)
    def _():
        at = F.at[pl.ds(1, blocks), planes + 1, pl.ds(SUB, rows)]
        pltpu.make_async_copy(at, at, halo_recv.at[1]).wait()

    @pl.when(area > 0)
    def _():
        pltpu.make_async_copy(edge_in.at[0], edge_in.at[0], halo_recv.at[3]).wait()
        for b in range(blocks):
            for k in range(planes):
                F[b + 1, k + 1, pl.ds(SUB - 1, 1), :] = edge_in[0, b, pl.ds(k, 1), :]

    @pl.when(area < n_area - 1)
    def _():
        pltpu.make_async_copy(edge_in.at[1], edge_in.at[1], halo_recv.at[2]).wait()
        for b in range(blocks):
            for k in range(planes):
                F[b + 1, k + 1, pl.ds(SUB + rows, 1), :] = edge_in[1, b, pl.ds(k, 1), :]

    @pl.when(area == 0)
    def _():
        for b in range(blocks):
            for k in range(planes):
                F[b + 1, k + 1, pl.ds(SUB - 1, 1), :] = zero[:1]

    @pl.when(area == n_area - 1)
    def _():
        for b in range(blocks):
            for k in range(planes):
                F[b + 1, k + 1, pl.ds(SUB + rows, 1), :] = zero[:1]

    def block(b, _):
        late = b // early

        @pl.when(b >= early)
        def _():
            wait_mat(b)

        def rest(t, _):
            interior(b, t * ((tiles - 1) - (tiles - 2) * late))
            return 0

        lax.fori_loop(0, 2 + inner * late, rest, 0)

        def finish(t, _):
            ends(b, 2 * t)
            ends(b, 2 * t + 1)
            return 0

        lax.fori_loop(0, tiles // 2, finish, 0)

        @pl.when(area < n_area - 1)
        def _():
            shear_copy(b).start()

        send_view(0, b)

        @pl.when(b > 0)
        def _():
            shear(b - 1)

        return 0

    lax.fori_loop(0, blocks, block, 0)
    shear(blocks - 1)

    for view in range(2):
        at = recv.at[view, :, pl.ds(0, n_depth - 1)]
        pltpu.make_async_copy(at, at, a2a_recv.at[view]).wait()

    low = sub_id < part
    for view in range(2):

        def compose(b, _):
            through = zero + 1.0
            total = [zero, zero]
            for k in range(n_depth):
                layer = order_s[view, k]
                one = recv[view, b, layer, pl.ds(0, SUB), :]
                two = recv[view, b, layer, pl.ds(SUB, SUB), :]
                total = [total[0] + through * one, total[1] + through * two]
                opacity = jnp.where(low, pltpu.roll(two, part, 0), two)
                through = through * (1.0 - opacity)
            columns_b = pl.ds(pl.multiple_of(b * LANES, LANES), LANES)
            out_ref[view, pl.ds(0, SUB), columns_b] = total[0]
            out_ref[view, pl.ds(SUB, SUB), columns_b] = total[1]
            return 0

        lax.fori_loop(0, blocks, compose, 0)

    for view in range(2):
        at = send.at[view, :, pl.ds(0, n_depth - 1)]
        pltpu.make_async_copy(at, at, a2a_send.at[view]).wait()

    @pl.when(area < n_area - 1)
    def _():
        for b in range(blocks):
            pltpu.make_async_copy(own.at[b], own.at[b], shear_send.at[b]).wait()
        pltpu.make_async_copy(edge_out.at[1], edge_out.at[1], halo_send.at[3]).wait()

    @pl.when(area > 0)
    def _():
        pltpu.make_async_copy(edge_out.at[0], edge_out.at[0], halo_send.at[2]).wait()

    @pl.when(depth < n_depth - 1)
    def _():
        at = F.at[pl.ds(1, blocks), 0, pl.ds(SUB, rows)]
        pltpu.make_async_copy(at, at, halo_send.at[0]).wait()

    @pl.when(depth > 0)
    def _():
        at = F.at[pl.ds(1, blocks), planes + 1, pl.ds(SUB, rows)]
        pltpu.make_async_copy(at, at, halo_send.at[1]).wait()


def solution(mesh):
    n_area, n_depth = mesh.shape["area"], mesh.shape["depth"]

    def shards(field, materials, tf_table, view_order, shear_offset):
        planes, rows, columns = field.shape
        blocks = columns // LANES
        part = rows // n_depth
        f32 = jnp.float32
        image = pl.pallas_call(
            functools.partial(kernel, n_area, n_depth),
            out_shape=jax.ShapeDtypeStruct((2, 4 * part, columns), f32),
            in_specs=[pl.BlockSpec(memory_space=pl.ANY)] * 5,
            out_specs=pl.BlockSpec(memory_space=pltpu.VMEM),
            scratch_shapes=[
                pltpu.VMEM((blocks + 2, planes + 2, rows + 2 * SUB, LANES), f32),
                pltpu.VMEM((blocks, planes, rows, LANES), jnp.int32),
                pltpu.SMEM(tf_table.shape, f32),
                pltpu.SMEM(view_order.shape, jnp.int32),
                pltpu.SMEM(shear_offset.shape, jnp.int32),
                pltpu.VMEM((2, blocks, planes, LANES), f32),
                pltpu.VMEM((2, blocks, planes, LANES), f32),
                pltpu.VMEM((blocks, 7, rows, LANES), f32),
                pltpu.VMEM((blocks, 4, rows, LANES), f32),
                pltpu.VMEM((blocks, 4, rows, LANES), f32),
                pltpu.VMEM((4, 2 * rows, LANES), f32),
                pltpu.VMEM((2, blocks, n_depth, 4 * part, LANES), f32),
                pltpu.VMEM((2, blocks, n_depth, 4 * part, LANES), f32),
                pltpu.SemaphoreType.DMA((2 * blocks,)),
                pltpu.SemaphoreType.DMA((3,)),
                pltpu.SemaphoreType.DMA((4,)),
                pltpu.SemaphoreType.DMA((4,)),
                pltpu.SemaphoreType.DMA((blocks,)),
                pltpu.SemaphoreType.DMA((blocks,)),
                pltpu.SemaphoreType.DMA((2,)),
                pltpu.SemaphoreType.DMA((2,)),
            ],
            compiler_params=pltpu.CompilerParams(
                collective_id=0, has_side_effects=True, vmem_limit_bytes=48 * 2**20
            ),
            name="render",
        )(field, materials, tf_table, view_order, shear_offset)
        return image.reshape(2, 4, part, columns)

    in_specs = (P("depth", "area", None), P("depth", "area", None), P(), P(), P())
    out_specs = P(None, None, ("area", "depth"), None)
    return jax.shard_map(shards, mesh=mesh, in_specs=in_specs, out_specs=out_specs, check_vma=False)
```

```python
import functools

import jax
import jax.numpy as jnp
from jax import lax
from jax.experimental import pallas as pl
from jax.experimental.pallas import tpu as pltpu
from jax.sharding import PartitionSpec as P

MESH = pl.DeviceIdType.MESH
LANES = 128
SUB = 8
EXP_SCALE = -0.25 * 1.4426950408889634


def sublane_gather(table, index):
    dims = lax.GatherDimensionNumbers(
        offset_dims=(),
        collapsed_slice_dims=(0,),
        start_index_map=(0,),
        operand_batching_dims=(1,),
        start_indices_batching_dims=(1,),
    )
    return lax.gather(
        table, index[..., None], dims, (1, 1), mode=lax.GatherScatterMode.PROMISE_IN_BOUNDS
    )


def kernel(
    n_area,
    n_depth,
    field_hbm,
    mat_hbm,
    tf_hbm,
    order_hbm,
    shear_hbm,
    out_ref,
    F,
    M,
    tf_s,
    order_s,
    shear_s,
    edge_out,
    edge_in,
    state,
    own,
    near,
    window,
    send,
    recv,
    load_sem,
    small_sem,
    plane_send,
    plane_recv,
    edge_send,
    edge_recv,
    shear_send,
    shear_recv,
    a2a_send,
    a2a_recv,
):
    planes, rows, columns = field_hbm.shape
    blocks = columns // LANES
    tiles = rows // SUB
    part = rows // n_depth
    halves = SUB // part
    area, depth = lax.axis_index("area"), lax.axis_index("depth")
    zero = jnp.zeros((SUB, LANES), jnp.float32)

    for b in range(blocks):
        pltpu.make_async_copy(
            field_hbm.at[:, :, pl.ds(b * LANES, LANES)],
            F.at[b + 1, pl.ds(1, planes), pl.ds(SUB, rows)],
            load_sem.at[b],
        ).start()
    for b in range(blocks):
        pltpu.make_async_copy(
            mat_hbm.at[:, :, pl.ds(b * LANES, LANES)], M.at[b], load_sem.at[blocks + b]
        ).start()
    small = [
        pltpu.make_async_copy(src, dst, small_sem.at[i])
        for i, (src, dst) in enumerate(
            ((tf_hbm, tf_s), (order_hbm, order_s), (shear_hbm, shear_s))
        )
    ]
    for copy in small:
        copy.start()

    def wait_field(b):
        pltpu.make_async_copy(
            F.at[b + 1, pl.ds(1, planes), pl.ds(SUB, rows)],
            F.at[b + 1, pl.ds(1, planes), pl.ds(SUB, rows)],
            load_sem.at[b],
        ).wait()

    def wait_mat(b):
        pltpu.make_async_copy(M.at[b], M.at[b], load_sem.at[blocks + b]).wait()

    barrier = pltpu.get_barrier_semaphore()

    def greet(i, _):
        peer = lax.rem(depth + i, n_depth)
        pl.semaphore_signal(barrier, inc=1, device_id={"depth": peer}, device_id_type=MESH)
        return 0

    lax.fori_loop(1, n_depth, greet, 0)

    @pl.when(area > 0)
    def _():
        pl.semaphore_signal(barrier, inc=1, device_id={"area": area - 1}, device_id_type=MESH)

    @pl.when(area < n_area - 1)
    def _():
        pl.semaphore_signal(barrier, inc=1, device_id={"area": area + 1}, device_id_type=MESH)

    def clear(k, _):
        for r in range(tiles + 2):
            F[0, k, pl.ds(r * SUB, SUB), :] = zero
            F[blocks + 1, k, pl.ds(r * SUB, SUB), :] = zero
        return 0

    lax.fori_loop(0, planes + 2, clear, 0)

    def clear_plane(at):
        for b in range(blocks):
            for r in range(tiles):
                F[b + 1, at, pl.ds(SUB + r * SUB, SUB), :] = zero

    for side, outer in ((0, area == 0), (1, area == n_area - 1)):

        @pl.when(outer)
        def _():
            for b in range(blocks):
                edge_in[side, b] = jnp.zeros((planes, LANES), jnp.float32)

    @pl.when(depth == 0)
    def _():
        clear_plane(0)

    @pl.when(depth == n_depth - 1)
    def _():
        clear_plane(planes + 1)

    def pack_edges():
        for b in range(blocks):
            wait_field(b)
        for b in range(blocks):
            for k in range(planes):
                edge_out[0, b, pl.ds(k, 1), :] = F[b + 1, k + 1, pl.ds(SUB, 1), :]
                edge_out[1, b, pl.ds(k, 1), :] = F[b + 1, k + 1, pl.ds(SUB + rows - 1, 1), :]

    for copy in small:
        copy.wait()
    sub_id = lax.broadcasted_iota(jnp.int32, (SUB, LANES), 0)
    lane_id = lax.broadcasted_iota(jnp.int32, (SUB, LANES), 1)
    is_first, is_last = lane_id == 0, lane_id == LANES - 1
    table = []
    for channel in range(4):
        pair = []
        for half in range(2):
            values = jnp.full((SUB, LANES), tf_s[channel, half * SUB], jnp.float32)
            for entry in range(1, SUB):
                values = jnp.where(sub_id == entry, tf_s[channel, half * SUB + entry], values)
            pair.append(values)
        table.append(pair)

    def cells(b, k, row):
        mid = pl.ds(pl.multiple_of(row + SUB, SUB), SUB)
        c = F[b + 1, k + 1, mid, :]
        gz = F[b + 1, k + 2, mid, :] - F[b + 1, k, mid, :]
        gy = F[b + 1, k + 1, pl.ds(row + SUB + 1, SUB), :] - F[b + 1, k + 1, pl.ds(row + SUB - 1, SUB), :]
        before = pltpu.roll(jnp.where(is_last, F[b, k + 1, mid, :], c), 1, 1)
        after = pltpu.roll(jnp.where(is_first, F[b + 2, k + 1, mid, :], c), LANES - 1, 1)
        gx = after - before
        gm2 = 0.25 * (gz * gz + gy * gy + gx * gx)
        lit = jnp.abs(0.168 * gz + 0.21 * gy + 0.224 * gx)
        shade = 0.3 + lit * lax.rsqrt(gm2 + 1.0)
        m = M[b, k, pl.ds(pl.multiple_of(row, SUB), SUB), :]
        upper, index = m > SUB - 1, m & (SUB - 1)
        looked = [
            jnp.where(upper, sublane_gather(hi, index), sublane_gather(lo, index))
            for lo, hi in table
        ]
        a = looked[3] * (1.0 - jnp.exp2(EXP_SCALE * (c * c + gm2)))
        return looked[:3], shade * a, 1.0 - a

    def march(b, tile, first, last):
        row = tile * SUB
        through = zero + 1.0
        front, back = [zero] * 3, [zero] * 3
        for k in range(first, last):
            colour, sa, keep = cells(b, k, row)
            weight = through * sa
            front = [f + t * weight for f, t in zip(front, colour)]
            back = [f * keep + t * sa for f, t in zip(back, colour)]
            through = through * keep
        return through, front, back

    def interior(b, tile):
        at = pl.ds(pl.multiple_of(tile * SUB, SUB), SUB)
        through, front, back = march(b, tile, 1, planes - 1)
        for i, value in enumerate([through, *front, *back]):
            state[b, i, at, :] = value

    def emit(b, tile, front, back, through):
        at = pl.ds(pl.multiple_of(tile * SUB, SUB), SUB)
        opacity = 1.0 - through
        for i, (first, second) in enumerate(zip([*front, opacity], [*back, opacity])):
            own[b, i, at, :] = second
            for half in range(halves):
                send[0, b, tile * halves + half, pl.ds(i * part, part), :] = first[
                    half * part : (half + 1) * part
                ]

        @pl.when(area < n_area - 1)
        def _():
            pltpu.make_async_remote_copy(
                src_ref=own.at[b, :, at],
                dst_ref=near.at[b, :, at],
                send_sem=shear_send.at[b],
                recv_sem=shear_recv.at[b],
                device_id={"area": area + 1},
                device_id_type=MESH,
            ).start()

        for half in range(halves):
            peer = tile * halves + half

            @pl.when(peer != depth)
            def _():
                part_copy(0, b, peer).start()

            @pl.when(peer == depth)
            def _():
                recv[0, b, depth] = send[0, b, depth]

    def full(b, tile):
        through, front, back = march(b, tile, 0, planes)
        emit(b, tile, front, back, through)

    def ends(b, tile):
        row = tile * SUB
        at = pl.ds(pl.multiple_of(row, SUB), SUB)
        colour0, sa0, keep0 = cells(b, 0, row)
        colour1, sa1, keep1 = cells(b, planes - 1, row)
        through = state[b, 0, at, :]
        front, back = [], []
        for i in range(3):
            c0, c1 = colour0[i] * sa0, colour1[i] * sa1
            front.append(c0 + keep0 * (state[b, 1 + i, at, :] + through * c1))
            back.append(c1 + keep1 * (state[b, 4 + i, at, :] + through * c0))
        emit(b, tile, front, back, through * keep0 * keep1)

    def part_copy(view, b, peer):
        return pltpu.make_async_remote_copy(
            src_ref=send.at[view, b, peer],
            dst_ref=recv.at[view, b, depth],
            send_sem=a2a_send.at[view],
            recv_sem=a2a_recv.at[view],
            device_id={"depth": peer},
            device_id_type=MESH,
        )

    offset = shear_s[depth]

    def shear(b):
        @pl.when(area > 0)
        def _():
            pltpu.make_async_copy(near.at[b], near.at[b], shear_recv.at[b]).wait()
            for i in range(4):
                window[i, pl.ds(0, rows), :] = near[b, i]

        for i in range(4):
            window[i, pl.ds(rows, rows), :] = own[b, i]
        for tile in range(tiles):
            for i in range(4):
                moved = window[i, pl.ds(rows + tile * SUB - offset, SUB), :]
                for half in range(halves):
                    send[1, b, tile * halves + half, pl.ds(i * part, part), :] = moved[
                        half * part : (half + 1) * part
                    ]

        def one(i, _):
            part_copy(1, b, lax.rem(depth + i, n_depth)).start()
            return 0

        lax.fori_loop(1, n_depth, one, 0)
        recv[1, b, depth] = send[1, b, depth]

    inner = tiles - 2
    ahead, early = depth * 0, 2

    def early_tile(i, _):
        b = i // inner
        tile = 1 + i % inner

        @pl.when(tile == 1)
        def _():
            wait_mat(b)

        interior(b, tile)
        return 0

    @pl.when(ahead > 0)
    def _():
        pack_edges()
        lax.fori_loop(0, ahead, early_tile, 0)

    @pl.when(jnp.logical_and(area > 0, area < n_area - 1))
    def _():
        pl.semaphore_wait(barrier, n_depth - 1 + 2)

    @pl.when(jnp.logical_or(area == 0, area == n_area - 1))
    def _():
        pl.semaphore_wait(barrier, n_depth - 1 + 1)

    def plane_copy(b, src, dst, way, peer):
        return pltpu.make_async_remote_copy(
            src_ref=field_hbm.at[src, :, pl.ds(b * LANES, LANES)],
            dst_ref=F.at[b + 1, dst, pl.ds(SUB, rows)],
            send_sem=plane_send.at[way],
            recv_sem=plane_recv.at[way, b],
            device_id={"depth": peer},
            device_id_type=MESH,
        )

    for b in range(blocks):

        @pl.when(depth < n_depth - 1)
        def _():
            plane_copy(b, planes - 1, 0, 0, depth + 1).start()

        @pl.when(depth > 0)
        def _():
            plane_copy(b, 0, planes + 1, 1, depth - 1).start()

    @pl.when(ahead == 0)
    def _():
        pack_edges()

    def edge_copy(side, peer):
        return pltpu.make_async_remote_copy(
            src_ref=edge_out.at[side],
            dst_ref=edge_in.at[1 - side],
            send_sem=edge_send.at[side],
            recv_sem=edge_recv.at[1 - side],
            device_id={"area": peer},
            device_id_type=MESH,
        )

    @pl.when(area < n_area - 1)
    def _():
        edge_copy(1, area + 1).start()

    @pl.when(area > 0)
    def _():
        edge_copy(0, area - 1).start()

    for i in range(4):

        @pl.when(area == 0)
        def _():
            for tile in range(tiles):
                window[i, pl.ds(tile * SUB, SUB), :] = zero

    lax.fori_loop(ahead, inner * early, early_tile, 0)

    for side, outer, at_row in ((0, area == 0, SUB - 1), (1, area == n_area - 1, SUB + rows)):

        @pl.when(jnp.logical_not(outer))
        def _():
            pltpu.make_async_copy(edge_in.at[side], edge_in.at[side], edge_recv.at[side]).wait()

        for b in range(blocks):
            for k in range(planes):
                value = edge_in[side, b, pl.ds(k, 1), :]
                F[b + 1, k + 1, pl.ds(at_row, 1), :] = value

    def block(b, _):
        late = jnp.where(b >= early, 1, 0)

        @pl.when(depth > 0)
        def _():
            at = F.at[b + 1, 0, pl.ds(SUB, rows)]
            pltpu.make_async_copy(at, at, plane_recv.at[0, b]).wait()

        @pl.when(depth < n_depth - 1)
        def _():
            at = F.at[b + 1, planes + 1, pl.ds(SUB, rows)]
            pltpu.make_async_copy(at, at, plane_recv.at[1, b]).wait()

        @pl.when(b >= early)
        def _():
            wait_mat(b)

        def rest(t, _):
            full(b, t * ((tiles - 1) - (tiles - 2) * late))
            return 0

        lax.fori_loop(0, 2 + inner * late, rest, 0)

        def finish(t, _):
            ends(b, 1 + 2 * t)
            ends(b, 2 + 2 * t)
            return 0

        lax.fori_loop(0, (inner // 2) * (1 - late), finish, 0)

        @pl.when(b > 0)
        def _():
            shear(b - 1)

        return 0

    lax.fori_loop(0, blocks, block, 0)
    shear(blocks - 1)

    for view in range(2):
        at = recv.at[view, :, pl.ds(0, n_depth - 1)]
        pltpu.make_async_copy(at, at, a2a_recv.at[view]).wait()

    low = sub_id < part
    for view in range(2):

        def compose(b, _):
            through = zero + 1.0
            total = [zero, zero]
            for k in range(n_depth):
                layer = order_s[view, k]
                one = recv[view, b, layer, pl.ds(0, SUB), :]
                two = recv[view, b, layer, pl.ds(SUB, SUB), :]
                total = [total[0] + through * one, total[1] + through * two]
                opacity = jnp.where(low, pltpu.roll(two, part, 0), two)
                through = through * (1.0 - opacity)
            columns_b = pl.ds(pl.multiple_of(b * LANES, LANES), LANES)
            out_ref[view, pl.ds(0, SUB), columns_b] = total[0]
            out_ref[view, pl.ds(SUB, SUB), columns_b] = total[1]
            return 0

        lax.fori_loop(0, blocks, compose, 0)

    for view in range(2):
        at = send.at[view, :, pl.ds(0, n_depth - 1)]
        pltpu.make_async_copy(at, at, a2a_send.at[view]).wait()

    @pl.when(area < n_area - 1)
    def _():
        for b in range(blocks):
            pltpu.make_async_copy(own.at[b], own.at[b], shear_send.at[b]).wait()
        pltpu.make_async_copy(edge_out.at[1], edge_out.at[1], edge_send.at[1]).wait()

    @pl.when(area > 0)
    def _():
        pltpu.make_async_copy(edge_out.at[0], edge_out.at[0], edge_send.at[0]).wait()

    @pl.when(depth < n_depth - 1)
    def _():
        at = F.at[pl.ds(1, blocks), 0, pl.ds(SUB, rows)]
        pltpu.make_async_copy(at, at, plane_send.at[0]).wait()

    @pl.when(depth > 0)
    def _():
        at = F.at[pl.ds(1, blocks), planes + 1, pl.ds(SUB, rows)]
        pltpu.make_async_copy(at, at, plane_send.at[1]).wait()


def solution(mesh):
    n_area, n_depth = mesh.shape["area"], mesh.shape["depth"]

    def shards(field, materials, tf_table, view_order, shear_offset):
        planes, rows, columns = field.shape
        blocks = columns // LANES
        part = rows // n_depth
        f32 = jnp.float32
        image = pl.pallas_call(
            functools.partial(kernel, n_area, n_depth),
            out_shape=jax.ShapeDtypeStruct((2, 4 * part, columns), f32),
            in_specs=[pl.BlockSpec(memory_space=pltpu.HBM)] * 5,
            out_specs=pl.BlockSpec(memory_space=pltpu.VMEM),
            scratch_shapes=[
                pltpu.VMEM((blocks + 2, planes + 2, rows + 2 * SUB, LANES), f32),
                pltpu.VMEM((blocks, planes, rows, LANES), jnp.int32),
                pltpu.SMEM(tf_table.shape, f32),
                pltpu.SMEM(view_order.shape, jnp.int32),
                pltpu.SMEM(shear_offset.shape, jnp.int32),
                pltpu.VMEM((2, blocks, planes, LANES), f32),
                pltpu.VMEM((2, blocks, planes, LANES), f32),
                pltpu.VMEM((blocks, 7, rows, LANES), f32),
                pltpu.VMEM((blocks, 4, rows, LANES), f32),
                pltpu.VMEM((blocks, 4, rows, LANES), f32),
                pltpu.VMEM((4, 2 * rows, LANES), f32),
                pltpu.VMEM((2, blocks, n_depth, 4 * part, LANES), f32),
                pltpu.VMEM((2, blocks, n_depth, 4 * part, LANES), f32),
                pltpu.SemaphoreType.DMA((2 * blocks,)),
                pltpu.SemaphoreType.DMA((3,)),
                pltpu.SemaphoreType.DMA((2,)),
                pltpu.SemaphoreType.DMA((2, blocks)),
                pltpu.SemaphoreType.DMA((2,)),
                pltpu.SemaphoreType.DMA((2,)),
                pltpu.SemaphoreType.DMA((blocks,)),
                pltpu.SemaphoreType.DMA((blocks,)),
                pltpu.SemaphoreType.DMA((2,)),
                pltpu.SemaphoreType.DMA((2,)),
            ],
            compiler_params=pltpu.CompilerParams(
                collective_id=0, has_side_effects=True, vmem_limit_bytes=60 * 2**20
            ),
            name="render",
        )(field, materials, tf_table, view_order, shear_offset)
        return image.reshape(2, 4, part, columns)

    in_specs = (P("depth", "area", None), P("depth", "area", None), P(), P(), P())
    out_specs = P(None, None, ("area", "depth"), None)
    return jax.shard_map(shards, mesh=mesh, in_specs=in_specs, out_specs=out_specs, check_vma=False)
```

```python
import functools

import jax
import jax.numpy as jnp
from jax import lax
from jax.experimental import pallas as pl
from jax.experimental.pallas import tpu as pltpu
from jax.sharding import PartitionSpec as P

MESH = pl.DeviceIdType.MESH
LANES = 128
SUB = 8
EXP_SCALE = -0.25 * 1.4426950408889634


def gather(table, index, axis):
    dims = lax.GatherDimensionNumbers(
        offset_dims=(),
        collapsed_slice_dims=(axis,),
        start_index_map=(axis,),
        operand_batching_dims=(1 - axis,),
        start_indices_batching_dims=(1 - axis,),
    )
    return lax.gather(
        table, index[..., None], dims, (1, 1), mode=lax.GatherScatterMode.PROMISE_IN_BOUNDS
    )


def kernel(
    n_area,
    n_depth,
    field_hbm,
    mat_hbm,
    tf_hbm,
    order_hbm,
    shear_hbm,
    out_ref,
    F,
    M,
    tf_s,
    order_s,
    shear_s,
    edge_out,
    edge_in,
    state,
    own,
    near,
    window,
    send,
    recv,
    final,
    load_sem,
    small_sem,
    plane_send,
    plane_recv,
    edge_send,
    edge_recv,
    shear_send,
    shear_recv,
    a2a_send,
    a2a_recv,
):
    planes, rows, columns = field_hbm.shape
    blocks = columns // LANES
    tiles = rows // SUB
    part = rows // n_depth
    halves = SUB // part
    last = blocks - 1
    area, depth = lax.axis_index("area"), lax.axis_index("depth")
    zero = jnp.zeros((SUB, LANES), jnp.float32)

    def load_field(b):
        pltpu.make_async_copy(
            field_hbm.at[:, :, pl.ds(b * LANES, LANES)],
            F.at[b + 1, pl.ds(1, planes), pl.ds(SUB, rows)],
            load_sem.at[b],
        ).start()

    load_field(0)
    for b in range(blocks):
        if b + 1 < blocks:
            load_field(b + 1)
        pltpu.make_async_copy(
            mat_hbm.at[:, :, pl.ds(b * LANES, LANES)], M.at[b], load_sem.at[blocks + b]
        ).start()
    small = [
        pltpu.make_async_copy(src, dst, small_sem.at[i])
        for i, (src, dst) in enumerate(
            ((tf_hbm, tf_s), (order_hbm, order_s), (shear_hbm, shear_s))
        )
    ]
    for copy in small:
        copy.start()

    def wait_field(b):
        pltpu.make_async_copy(
            F.at[b + 1, pl.ds(1, planes), pl.ds(SUB, rows)],
            F.at[b + 1, pl.ds(1, planes), pl.ds(SUB, rows)],
            load_sem.at[b],
        ).wait()

    def wait_mat(b):
        pltpu.make_async_copy(M.at[b], M.at[b], load_sem.at[blocks + b]).wait()

    barrier = pltpu.get_barrier_semaphore()

    def greet(i, _):
        peer = lax.rem(depth + i, n_depth)
        pl.semaphore_signal(barrier, inc=1, device_id={"depth": peer}, device_id_type=MESH)
        return 0

    lax.fori_loop(1, n_depth, greet, 0)

    @pl.when(area > 0)
    def _():
        pl.semaphore_signal(barrier, inc=1, device_id={"area": area - 1}, device_id_type=MESH)

    @pl.when(area < n_area - 1)
    def _():
        pl.semaphore_signal(barrier, inc=1, device_id={"area": area + 1}, device_id_type=MESH)

    def clear(k, _):
        for r in range(tiles + 2):
            F[0, k, pl.ds(r * SUB, SUB), :] = zero
            F[blocks + 1, k, pl.ds(r * SUB, SUB), :] = zero
        return 0

    lax.fori_loop(0, planes + 2, clear, 0)

    def clear_plane(at):
        for b in range(blocks):
            for r in range(tiles):
                F[b + 1, at, pl.ds(SUB + r * SUB, SUB), :] = zero

    for side, outer in ((0, area == 0), (1, area == n_area - 1)):

        @pl.when(outer)
        def _():
            for b in range(blocks):
                edge_in[side, b] = jnp.zeros((planes, LANES), jnp.float32)

    @pl.when(depth == 0)
    def _():
        clear_plane(0)

    @pl.when(depth == n_depth - 1)
    def _():
        clear_plane(planes + 1)

    def pack_edges(b):
        for k in range(planes):
            edge_out[0, b, pl.ds(k, 1), :] = F[b + 1, k + 1, pl.ds(SUB, 1), :]
            edge_out[1, b, pl.ds(k, 1), :] = F[b + 1, k + 1, pl.ds(SUB + rows - 1, 1), :]

    for copy in small:
        copy.wait()
    sub_id = lax.broadcasted_iota(jnp.int32, (SUB, LANES), 0)
    lane_id = lax.broadcasted_iota(jnp.int32, (SUB, LANES), 1)
    is_first, is_last = lane_id == 0, lane_id == LANES - 1
    table = []
    for channel in range(3):
        pair = []
        for half in range(2):
            values = jnp.full((SUB, LANES), tf_s[channel, half * SUB], jnp.float32)
            for entry in range(1, SUB):
                values = jnp.where(sub_id == entry, tf_s[channel, half * SUB + entry], values)
            pair.append(values)
        table.append(pair)
    opacities = jnp.zeros((SUB, LANES), jnp.float32)
    for entry in range(tf_s.shape[1]):
        opacities = jnp.where(lane_id == entry, tf_s[3, entry], opacities)

    def cells(b, k, row):
        mid = pl.ds(pl.multiple_of(row + SUB, SUB), SUB)
        c = F[b + 1, k + 1, mid, :]
        gz = F[b + 1, k + 2, mid, :] - F[b + 1, k, mid, :]
        gy = F[b + 1, k + 1, pl.ds(row + SUB + 1, SUB), :] - F[b + 1, k + 1, pl.ds(row + SUB - 1, SUB), :]
        before = pltpu.roll(jnp.where(is_last, F[b, k + 1, mid, :], c), 1, 1)
        after = pltpu.roll(jnp.where(is_first, F[b + 2, k + 1, mid, :], c), LANES - 1, 1)
        gx = after - before
        gm2 = 0.25 * (gz * gz + gy * gy + gx * gx)
        lit = jnp.abs(0.168 * gz + 0.21 * gy + 0.224 * gx)
        shade = 0.3 + lit * lax.rsqrt(gm2 + 1.0)
        m = M[b, k, pl.ds(pl.multiple_of(row, SUB), SUB), :]
        upper, index = m > SUB - 1, m & (SUB - 1)
        looked = [
            jnp.where(upper, gather(hi, index, 0), gather(lo, index, 0))
            for lo, hi in table
        ]
        a = gather(opacities, m, 1) * (1.0 - jnp.exp2(EXP_SCALE * (c * c + gm2)))
        return looked, shade * a, 1.0 - a

    def march(b, tile, first, last):
        row = tile * SUB
        through = zero + 1.0
        front, back = [zero] * 3, [zero] * 3
        for k in range(first, last):
            colour, sa, keep = cells(b, k, row)
            colour = [t * sa for t in colour]
            front = [f + c * through for f, c in zip(front, colour)]
            back = [f * keep + c for f, c in zip(back, colour)]
            through = through * keep
        return through, front, back

    def interior(b, tile):
        at = pl.ds(pl.multiple_of(tile * SUB, SUB), SUB)
        through, front, back = march(b, tile, 1, planes - 1)
        for i, value in enumerate([through, *front, *back]):
            state[b, i, at, :] = value

    def emit(b, tile, front, back, through):
        at = pl.ds(pl.multiple_of(tile * SUB, SUB), SUB)
        opacity = 1.0 - through
        for i, (first, second) in enumerate(zip([*front, opacity], [*back, opacity])):
            own[b, i, at, :] = second
            for half in range(halves):
                send[0, b, tile * halves + half, pl.ds(i * part, part), :] = first[
                    half * part : (half + 1) * part
                ]

        @pl.when(area < n_area - 1)
        def _():
            pltpu.make_async_remote_copy(
                src_ref=own.at[b, :, at],
                dst_ref=near.at[b, :, at],
                send_sem=shear_send.at[b],
                recv_sem=shear_recv.at[b],
                device_id={"area": area + 1},
                device_id_type=MESH,
            ).start()

        for half in range(halves):
            peer = tile * halves + half

            @pl.when(peer != depth)
            def _():
                part_copy(0, b, peer).start()

            @pl.when(peer == depth)
            def _():
                recv[0, b, depth] = send[0, b, depth]

    def full(b, tile):
        through, front, back = march(b, tile, 0, planes)
        emit(b, tile, front, back, through)

    def ends(b, tile):
        row = tile * SUB
        at = pl.ds(pl.multiple_of(row, SUB), SUB)
        colour0, sa0, keep0 = cells(b, 0, row)
        colour1, sa1, keep1 = cells(b, planes - 1, row)
        through = state[b, 0, at, :]
        front, back = [], []
        for i in range(3):
            c0, c1 = colour0[i] * sa0, colour1[i] * sa1
            front.append(c0 + keep0 * (state[b, 1 + i, at, :] + through * c1))
            back.append(c1 + keep1 * (state[b, 4 + i, at, :] + through * c0))
        emit(b, tile, front, back, through * keep0 * keep1)

    def part_copy(view, b, peer):
        return pltpu.make_async_remote_copy(
            src_ref=send.at[view, b, peer],
            dst_ref=recv.at[view, b, depth],
            send_sem=a2a_send.at[view],
            recv_sem=a2a_recv.at[view],
            device_id={"depth": peer},
            device_id_type=MESH,
        )

    offset = shear_s[depth]

    edge = int(n_depth**0.5)
    far = sorted(
        ((x, z) for x in range(edge) for z in range(edge) if x or z),
        key=lambda p: -min(p[0], edge - p[0]) - min(p[1], edge - p[1]),
    )

    def peer_at(x, z):
        return lax.rem(depth // edge + x, edge) * edge + lax.rem(depth + z, edge)

    def shear(b, place, slot, sems):
        @pl.when(area > 0)
        def _():
            pltpu.make_async_copy(near.at[b], near.at[b], shear_recv.at[b]).wait()
            for i in range(4):
                window[i, pl.ds(0, rows), :] = near[b, i]

        for i in range(4):
            window[i, pl.ds(rows, rows), :] = own[b, i]
        for tile in range(tiles):
            for i in range(4):
                moved = window[i, pl.ds(rows + tile * SUB - offset, SUB), :]
                for half in range(halves):
                    send[1, b, tile * halves + half, pl.ds(i * part, part), :] = moved[
                        half * part : (half + 1) * part
                    ]

        for x, z in far:
            peer = peer_at(x, z)
            pltpu.make_async_remote_copy(
                src_ref=send.at[1, b, peer],
                dst_ref=place.at[slot[0], slot[1], depth],
                send_sem=a2a_send.at[1],
                recv_sem=sems,
                device_id={"depth": peer},
                device_id_type=MESH,
            ).start()
        place[slot[0], slot[1], depth] = send[1, b, depth]

    inner = tiles - 2
    early = 2

    def plane_copy(b, src, dst, way, peer):
        return pltpu.make_async_remote_copy(
            src_ref=field_hbm.at[src, :, pl.ds(b * LANES, LANES)],
            dst_ref=F.at[b + 1, dst, pl.ds(SUB, rows)],
            send_sem=plane_send.at[way],
            recv_sem=plane_recv.at[way, b],
            device_id={"depth": peer},
            device_id_type=MESH,
        )

    def send_planes(b):
        @pl.when(depth < n_depth - 1)
        def _():
            plane_copy(b, planes - 1, 0, 0, depth + 1).start()

        @pl.when(depth > 0)
        def _():
            plane_copy(b, 0, planes + 1, 1, depth - 1).start()

    def edge_copy(b, side, peer):
        return pltpu.make_async_remote_copy(
            src_ref=edge_out.at[side, b],
            dst_ref=edge_in.at[1 - side, b],
            send_sem=edge_send.at[side],
            recv_sem=edge_recv.at[1 - side, b],
            device_id={"area": peer},
            device_id_type=MESH,
        )

    def send_edges(b):
        pack_edges(b)

        @pl.when(area < n_area - 1)
        def _():
            edge_copy(b, 1, area + 1).start()

        @pl.when(area > 0)
        def _():
            edge_copy(b, 0, area - 1).start()

    def early_tile(i, _):
        b = i // inner
        tile = 1 + i % inner

        @pl.when(tile == 1)
        def _():
            wait_mat(b)

        interior(b, tile)
        return 0

    def early_tile_and_halo(i, _):
        for b in range(1, blocks):

            @pl.when(i == 2 * b - 1)
            def _():
                send_planes(b)
                if b > 1:
                    wait_field(b)
                send_edges(b)

        return early_tile(i, 0)

    @pl.when(jnp.logical_and(area > 0, area < n_area - 1))
    def _():
        pl.semaphore_wait(barrier, n_depth - 1 + 2)

    @pl.when(jnp.logical_or(area == 0, area == n_area - 1))
    def _():
        pl.semaphore_wait(barrier, n_depth - 1 + 1)

    send_planes(0)

    wait_field(0)
    wait_field(1)
    send_edges(0)

    @pl.when(area == 0)
    def _():
        for i in range(4):
            for tile in range(tiles):
                window[i, pl.ds(tile * SUB, SUB), :] = zero

    lax.fori_loop(0, inner * early, early_tile_and_halo, 0)

    def block(b, _):
        late = jnp.where(b >= early, 1, 0)

        for side, outer, at_row in ((0, area == 0, SUB - 1), (1, area == n_area - 1, SUB + rows)):

            @pl.when(jnp.logical_not(outer))
            def _():
                at = edge_in.at[side, b]
                pltpu.make_async_copy(at, at, edge_recv.at[side, b]).wait()

            for k in range(planes):
                value = edge_in[side, b, pl.ds(k, 1), :]
                F[b + 1, k + 1, pl.ds(at_row, 1), :] = value

        @pl.when(depth > 0)
        def _():
            at = F.at[b + 1, 0, pl.ds(SUB, rows)]
            pltpu.make_async_copy(at, at, plane_recv.at[0, b]).wait()

        @pl.when(depth < n_depth - 1)
        def _():
            at = F.at[b + 1, planes + 1, pl.ds(SUB, rows)]
            pltpu.make_async_copy(at, at, plane_recv.at[1, b]).wait()

        @pl.when(b >= early)
        def _():
            wait_mat(b)

        def rest(t, _):
            full(b, t * ((tiles - 1) - (tiles - 2) * late))
            return 0

        lax.fori_loop(0, 2 + inner * late, rest, 0)

        def finish(t, _):
            ends(b, 1 + 2 * t)
            ends(b, 2 + 2 * t)
            return 0

        lax.fori_loop(0, (inner // 2) * (1 - late), finish, 0)

        @pl.when(b > 0)
        def _():
            shear(b - 1, recv, (1, b - 1), a2a_recv.at[1])

        return 0

    lax.fori_loop(0, blocks, block, 0)
    shear(last, final, (0, 0), a2a_recv.at[2])

    low = sub_id < part

    def compose(view, b, held):
        through = zero + 1.0
        total = [zero, zero]
        for k in range(n_depth):
            layer = order_s[view, k]
            one, two = [held[view, b, layer, pl.ds(h * SUB, SUB), :] for h in range(2)]
            total = [total[0] + through * one, total[1] + through * two]
            opacity = jnp.where(low, pltpu.roll(two, part, 0), two)
            through = through * (1.0 - opacity)
        return total

    def compose_last():
        through = zero + 1.0
        total = [zero, zero]
        for k in range(n_depth):
            layer = order_s[1, k]
            one, two = [final[0, 0, layer, pl.ds(h * SUB, SUB), :] for h in range(2)]
            total = [total[0] + through * one, total[1] + through * two]
            opacity = jnp.where(low, pltpu.roll(two, part, 0), two)
            through = through * (1.0 - opacity)
        return total

    def put(view, b, total):
        columns_b = pl.ds(pl.multiple_of(b * LANES, LANES), LANES)
        out_ref[view, pl.ds(0, SUB), columns_b] = total[0]
        out_ref[view, pl.ds(SUB, SUB), columns_b] = total[1]

    for view, count in ((1, last), (0, blocks)):
        at = recv.at[view, pl.ds(0, count), pl.ds(0, n_depth - 1)]
        pltpu.make_async_copy(at, at, a2a_recv.at[view]).wait()

    def some(b, _):
        for view in range(2):
            put(view, b, compose(view, b, recv))
        return 0

    lax.fori_loop(0, last, some, 0)
    put(0, last, compose(0, last, recv))

    at = final.at[0, 0, pl.ds(0, n_depth - 1)]
    pltpu.make_async_copy(at, at, a2a_recv.at[2]).wait()
    put(1, last, compose_last())

    for view in range(2):
        at = send.at[view, :, pl.ds(0, n_depth - 1)]
        pltpu.make_async_copy(at, at, a2a_send.at[view]).wait()

    @pl.when(area < n_area - 1)
    def _():
        for b in range(blocks):
            pltpu.make_async_copy(own.at[b], own.at[b], shear_send.at[b]).wait()
        pltpu.make_async_copy(edge_out.at[1], edge_out.at[1], edge_send.at[1]).wait()

    @pl.when(area > 0)
    def _():
        pltpu.make_async_copy(edge_out.at[0], edge_out.at[0], edge_send.at[0]).wait()

    @pl.when(depth < n_depth - 1)
    def _():
        at = F.at[pl.ds(1, blocks), 0, pl.ds(SUB, rows)]
        pltpu.make_async_copy(at, at, plane_send.at[0]).wait()

    @pl.when(depth > 0)
    def _():
        at = F.at[pl.ds(1, blocks), planes + 1, pl.ds(SUB, rows)]
        pltpu.make_async_copy(at, at, plane_send.at[1]).wait()


def solution(mesh):
    n_area, n_depth = mesh.shape["area"], mesh.shape["depth"]

    def shards(field, materials, tf_table, view_order, shear_offset):
        planes, rows, columns = field.shape
        blocks = columns // LANES
        part = rows // n_depth
        f32 = jnp.float32
        image = pl.pallas_call(
            functools.partial(kernel, n_area, n_depth),
            out_shape=jax.ShapeDtypeStruct((2, 4 * part, columns), f32),
            in_specs=[pl.BlockSpec(memory_space=pltpu.HBM)] * 5,
            out_specs=pl.BlockSpec(memory_space=pltpu.VMEM),
            scratch_shapes=[
                pltpu.VMEM((blocks + 2, planes + 2, rows + 2 * SUB, LANES), f32),
                pltpu.VMEM((blocks, planes, rows, LANES), jnp.int32),
                pltpu.SMEM(tf_table.shape, f32),
                pltpu.SMEM(view_order.shape, jnp.int32),
                pltpu.SMEM(shear_offset.shape, jnp.int32),
                pltpu.VMEM((2, blocks, planes, LANES), f32),
                pltpu.VMEM((2, blocks, planes, LANES), f32),
                pltpu.VMEM((blocks, 7, rows, LANES), f32),
                pltpu.VMEM((blocks, 4, rows, LANES), f32),
                pltpu.VMEM((blocks, 4, rows, LANES), f32),
                pltpu.VMEM((4, 2 * rows, LANES), f32),
                pltpu.VMEM((2, blocks, n_depth, 4 * part, LANES), f32),
                pltpu.VMEM((2, blocks, n_depth, 4 * part, LANES), f32),
                pltpu.VMEM((1, 1, n_depth, 4 * part, LANES), f32),
                pltpu.SemaphoreType.DMA((2 * blocks,)),
                pltpu.SemaphoreType.DMA((3,)),
                pltpu.SemaphoreType.DMA((2,)),
                pltpu.SemaphoreType.DMA((2, blocks)),
                pltpu.SemaphoreType.DMA((2,)),
                pltpu.SemaphoreType.DMA((2, blocks)),
                pltpu.SemaphoreType.DMA((blocks,)),
                pltpu.SemaphoreType.DMA((blocks,)),
                pltpu.SemaphoreType.DMA((2,)),
                pltpu.SemaphoreType.DMA((3,)),
            ],
            compiler_params=pltpu.CompilerParams(
                collective_id=0, has_side_effects=True, vmem_limit_bytes=60 * 2**20
            ),
            name="render",
        )(field, materials, tf_table, view_order, shear_offset)
        return image.reshape(2, 4, part, columns)

    in_specs = (P("depth", "area", None), P("depth", "area", None), P(), P(), P())
    out_specs = P(None, None, ("area", "depth"), None)
    return jax.shard_map(shards, mesh=mesh, in_specs=in_specs, out_specs=out_specs, check_vma=False)
```

```python
import functools

import jax
import jax.numpy as jnp
from jax import lax
from jax.experimental import pallas as pl
from jax.experimental.pallas import tpu as pltpu
from jax.sharding import PartitionSpec as P

MESH = pl.DeviceIdType.MESH
LANES = 128
SUB = 8
LIGHT = 0.7 * 0.24
EXP_SCALE = -0.25 * 1.4426950408889634


def gather(table, index, axis):
    dims = lax.GatherDimensionNumbers(
        offset_dims=(),
        collapsed_slice_dims=(axis,),
        start_index_map=(axis,),
        operand_batching_dims=(1 - axis,),
        start_indices_batching_dims=(1 - axis,),
    )
    return lax.gather(
        table, index[..., None], dims, (1, 1), mode=lax.GatherScatterMode.PROMISE_IN_BOUNDS
    )


def kernel(
    n_area,
    n_depth,
    field_hbm,
    mat_hbm,
    tf_hbm,
    order_hbm,
    shear_hbm,
    out_ref,
    F,
    M,
    tf_s,
    order_s,
    shear_s,
    edge_out,
    edge_in,
    state,
    own,
    near,
    window,
    send,
    recv,
    final,
    load_sem,
    small_sem,
    plane_send,
    plane_recv,
    edge_send,
    edge_recv,
    shear_send,
    shear_recv,
    a2a_send,
    a2a_recv,
):
    planes, rows, columns = field_hbm.shape
    blocks = columns // LANES
    tiles = rows // SUB
    part = rows // n_depth
    halves = SUB // part
    last = blocks - 1
    area, depth = lax.axis_index("area"), lax.axis_index("depth")
    zero = jnp.zeros((SUB, LANES), jnp.float32)

    def load_field(b):
        pltpu.make_async_copy(
            field_hbm.at[:, :, pl.ds(b * LANES, LANES)],
            F.at[b + 1, pl.ds(1, planes), pl.ds(SUB, rows)],
            load_sem.at[b],
        ).start()

    load_field(0)
    for b in range(blocks):
        if b + 1 < blocks:
            load_field(b + 1)
        pltpu.make_async_copy(
            mat_hbm.at[:, :, pl.ds(b * LANES, LANES)], M.at[b], load_sem.at[blocks + b]
        ).start()
    small = [
        pltpu.make_async_copy(src, dst, small_sem.at[i])
        for i, (src, dst) in enumerate(
            ((tf_hbm, tf_s), (order_hbm, order_s), (shear_hbm, shear_s))
        )
    ]
    for copy in small:
        copy.start()

    def wait_field(b):
        pltpu.make_async_copy(
            F.at[b + 1, pl.ds(1, planes), pl.ds(SUB, rows)],
            F.at[b + 1, pl.ds(1, planes), pl.ds(SUB, rows)],
            load_sem.at[b],
        ).wait()

    def wait_mat(b):
        pltpu.make_async_copy(M.at[b], M.at[b], load_sem.at[blocks + b]).wait()

    barrier = pltpu.get_barrier_semaphore()

    def greet(i, _):
        peer = lax.rem(depth + i, n_depth)
        pl.semaphore_signal(barrier, inc=1, device_id={"depth": peer}, device_id_type=MESH)
        return 0

    lax.fori_loop(1, n_depth, greet, 0)

    @pl.when(area > 0)
    def _():
        pl.semaphore_signal(barrier, inc=1, device_id={"area": area - 1}, device_id_type=MESH)

    @pl.when(area < n_area - 1)
    def _():
        pl.semaphore_signal(barrier, inc=1, device_id={"area": area + 1}, device_id_type=MESH)

    def clear(k, _):
        for r in range(tiles + 2):
            F[0, k, pl.ds(r * SUB, SUB), :] = zero
            F[blocks + 1, k, pl.ds(r * SUB, SUB), :] = zero
        return 0

    lax.fori_loop(0, planes + 2, clear, 0)

    def clear_plane(at):
        for b in range(blocks):
            for r in range(tiles):
                F[b + 1, at, pl.ds(SUB + r * SUB, SUB), :] = zero

    for side, outer in ((0, area == 0), (1, area == n_area - 1)):

        @pl.when(outer)
        def _():
            for b in range(blocks):
                edge_in[side, b] = jnp.zeros((planes, LANES), jnp.float32)

    @pl.when(depth == 0)
    def _():
        clear_plane(0)

    @pl.when(depth == n_depth - 1)
    def _():
        clear_plane(planes + 1)

    def pack_edges(b):
        for k in range(planes):
            edge_out[0, b, pl.ds(k, 1), :] = F[b + 1, k + 1, pl.ds(SUB, 1), :]
            edge_out[1, b, pl.ds(k, 1), :] = F[b + 1, k + 1, pl.ds(SUB + rows - 1, 1), :]

    for copy in small:
        copy.wait()
    sub_id = lax.broadcasted_iota(jnp.int32, (SUB, LANES), 0)
    lane_id = lax.broadcasted_iota(jnp.int32, (SUB, LANES), 1)
    is_first, is_last = lane_id == 0, lane_id == LANES - 1
    table = []
    for channel in range(3):
        pair = []
        for half in range(2):
            values = jnp.full((SUB, LANES), tf_s[channel, half * SUB], jnp.float32)
            for entry in range(1, SUB):
                values = jnp.where(sub_id == entry, tf_s[channel, half * SUB + entry], values)
            pair.append(values)
        table.append([LIGHT * values for values in pair])
    opacities = jnp.zeros((SUB, LANES), jnp.float32)
    for entry in range(tf_s.shape[1]):
        opacities = jnp.where(lane_id == entry, tf_s[3, entry], opacities)

    def cells(b, k, row):
        mid = pl.ds(pl.multiple_of(row + SUB, SUB), SUB)
        c = F[b + 1, k + 1, mid, :]
        gz = F[b + 1, k + 2, mid, :] - F[b + 1, k, mid, :]
        gy = F[b + 1, k + 1, pl.ds(row + SUB + 1, SUB), :] - F[b + 1, k + 1, pl.ds(row + SUB - 1, SUB), :]
        before = pltpu.roll(jnp.where(is_last, F[b, k + 1, mid, :], c), 1, 1)
        after = pltpu.roll(jnp.where(is_first, F[b + 2, k + 1, mid, :], c), LANES - 1, 1)
        gx = after - before
        gm2 = 0.25 * (gz * gz + gy * gy + gx * gx)
        lit = jnp.abs(gz + (0.3 / 0.24) * gy + (0.32 / 0.24) * gx)
        shade = 0.3 / LIGHT + lit * lax.rsqrt(gm2 + 1.0)
        m = M[b, k, pl.ds(pl.multiple_of(row, SUB), SUB), :]
        upper, index = m > SUB - 1, m & (SUB - 1)
        looked = [
            jnp.where(upper, gather(hi, index, 0), gather(lo, index, 0))
            for lo, hi in table
        ]
        a = gather(opacities, m, 1) * (1.0 - jnp.exp2(EXP_SCALE * (c * c + gm2)))
        return looked, shade * a, 1.0 - a

    def march(b, tile, first, last):
        row = tile * SUB
        through = zero + 1.0
        front, back = [zero] * 3, [zero] * 3
        for k in range(first, last):
            colour, sa, keep = cells(b, k, row)
            colour = [t * sa for t in colour]
            front = [f + c * through for f, c in zip(front, colour)]
            back = [f * keep + c for f, c in zip(back, colour)]
            through = through * keep
        return through, front, back

    def interior(b, several):
        marched = [march(b, tile, 1, planes - 1) for tile in several]
        for tile, (through, front, back) in zip(several, marched):
            at = pl.ds(pl.multiple_of(tile * SUB, SUB), SUB)
            for i, value in enumerate([through, *front, *back]):
                state[b, i, at, :] = value

    def keep(b, tile, front, back, through):
        at = pl.ds(pl.multiple_of(tile * SUB, SUB), SUB)
        opacity = 1.0 - through
        for i, (first, second) in enumerate(zip([*front, opacity], [*back, opacity])):
            own[b, i, at, :] = second
            for half in range(halves):
                send[0, b, tile * halves + half, pl.ds(i * part, part), :] = first[
                    half * part : (half + 1) * part
                ]

    def leave(b, tile):
        at = pl.ds(pl.multiple_of(tile * SUB, SUB), SUB)

        @pl.when(area < n_area - 1)
        def _():
            pltpu.make_async_remote_copy(
                src_ref=own.at[b, :, at],
                dst_ref=near.at[b, :, at],
                send_sem=shear_send.at[b],
                recv_sem=shear_recv.at[b],
                device_id={"area": area + 1},
                device_id_type=MESH,
            ).start()

        for half in range(halves):
            peer = tile * halves + half

            @pl.when(peer != depth)
            def _():
                part_copy(0, b, peer).start()

            @pl.when(peer == depth)
            def _():
                recv[0, b, depth] = send[0, b, depth]

    def full(b, several):
        marched = [march(b, tile, 0, planes) for tile in several]
        for tile, (through, front, back) in zip(several, marched):
            keep(b, tile, front, back, through)
        for tile in several:
            leave(b, tile)

    def ends(b, several):
        for tile in several:
            row = tile * SUB
            at = pl.ds(pl.multiple_of(row, SUB), SUB)
            colour0, sa0, keep0 = cells(b, 0, row)
            colour1, sa1, keep1 = cells(b, planes - 1, row)
            through = state[b, 0, at, :]
            front, back = [], []
            for i in range(3):
                c0, c1 = colour0[i] * sa0, colour1[i] * sa1
                front.append(c0 + keep0 * (state[b, 1 + i, at, :] + through * c1))
                back.append(c1 + keep1 * (state[b, 4 + i, at, :] + through * c0))
            keep(b, tile, front, back, through * keep0 * keep1)
        for tile in several:
            leave(b, tile)

    def part_copy(view, b, peer):
        return pltpu.make_async_remote_copy(
            src_ref=send.at[view, b, peer],
            dst_ref=recv.at[view, b, depth],
            send_sem=a2a_send.at[view],
            recv_sem=a2a_recv.at[view],
            device_id={"depth": peer},
            device_id_type=MESH,
        )

    offset = shear_s[depth]

    edge = int(n_depth**0.5)
    far = sorted(
        ((x, z) for x in range(edge) for z in range(edge) if x or z),
        key=lambda p: -min(p[0], edge - p[0]) - min(p[1], edge - p[1]),
    )

    def peer_at(x, z):
        return lax.rem(depth // edge + x, edge) * edge + lax.rem(depth + z, edge)

    def shear(b, place, slot, sems):
        @pl.when(area > 0)
        def _():
            pltpu.make_async_copy(near.at[b], near.at[b], shear_recv.at[b]).wait()
            for i in range(4):
                window[i, pl.ds(0, rows), :] = near[b, i]

        for i in range(4):
            window[i, pl.ds(rows, rows), :] = own[b, i]
        for tile in range(tiles):
            for i in range(4):
                moved = window[i, pl.ds(rows + tile * SUB - offset, SUB), :]
                for half in range(halves):
                    send[1, b, tile * halves + half, pl.ds(i * part, part), :] = moved[
                        half * part : (half + 1) * part
                    ]

        for x, z in far:
            peer = peer_at(x, z)
            pltpu.make_async_remote_copy(
                src_ref=send.at[1, b, peer],
                dst_ref=place.at[slot[0], slot[1], depth],
                send_sem=a2a_send.at[1],
                recv_sem=sems,
                device_id={"depth": peer},
                device_id_type=MESH,
            ).start()
        place[slot[0], slot[1], depth] = send[1, b, depth]

    inner = tiles - 2
    early = 2

    def plane_copy(b, src, dst, way, peer):
        return pltpu.make_async_remote_copy(
            src_ref=F.at[b + 1, src + 1, pl.ds(SUB, rows)],
            dst_ref=F.at[b + 1, dst, pl.ds(SUB, rows)],
            send_sem=plane_send.at[way],
            recv_sem=plane_recv.at[way, b],
            device_id={"depth": peer},
            device_id_type=MESH,
        )

    def send_planes(b):
        @pl.when(depth < n_depth - 1)
        def _():
            plane_copy(b, planes - 1, 0, 0, depth + 1).start()

        @pl.when(depth > 0)
        def _():
            plane_copy(b, 0, planes + 1, 1, depth - 1).start()

    def edge_copy(b, side, peer):
        return pltpu.make_async_remote_copy(
            src_ref=edge_out.at[side, b],
            dst_ref=edge_in.at[1 - side, b],
            send_sem=edge_send.at[side],
            recv_sem=edge_recv.at[1 - side, b],
            device_id={"area": peer},
            device_id_type=MESH,
        )

    def send_edges(b):
        pack_edges(b)

        @pl.when(area < n_area - 1)
        def _():
            edge_copy(b, 1, area + 1).start()

        @pl.when(area > 0)
        def _():
            edge_copy(b, 0, area - 1).start()

    def early_tile(i, _):
        b = i // (inner // 3)
        tile = 1 + 3 * (i % (inner // 3))

        @pl.when(tile == 1)
        def _():
            wait_mat(b)

        interior(b, [tile + j for j in range(3)])
        return 0

    def early_tile_and_halo(i, _):
        for b in range(1, blocks):

            @pl.when(i == b - 1)
            def _():
                if b > 1:
                    wait_field(b)
                send_planes(b)
                send_edges(b)

        return early_tile(i, 0)

    @pl.when(jnp.logical_and(area > 0, area < n_area - 1))
    def _():
        pl.semaphore_wait(barrier, n_depth - 1 + 2)

    @pl.when(jnp.logical_or(area == 0, area == n_area - 1))
    def _():
        pl.semaphore_wait(barrier, n_depth - 1 + 1)

    wait_field(0)
    send_planes(0)
    wait_field(1)
    send_edges(0)

    @pl.when(area == 0)
    def _():
        for i in range(4):
            for tile in range(tiles):
                window[i, pl.ds(tile * SUB, SUB), :] = zero

    lax.fori_loop(0, (inner // 3) * early, early_tile_and_halo, 0)

    def block(b, _):
        late = jnp.where(b >= early, 1, 0)

        for side, outer, at_row in ((0, area == 0, SUB - 1), (1, area == n_area - 1, SUB + rows)):

            @pl.when(jnp.logical_not(outer))
            def _():
                at = edge_in.at[side, b]
                pltpu.make_async_copy(at, at, edge_recv.at[side, b]).wait()

            for k in range(planes):
                value = edge_in[side, b, pl.ds(k, 1), :]
                F[b + 1, k + 1, pl.ds(at_row, 1), :] = value

        @pl.when(depth > 0)
        def _():
            at = F.at[b + 1, 0, pl.ds(SUB, rows)]
            pltpu.make_async_copy(at, at, plane_recv.at[0, b]).wait()

        @pl.when(depth < n_depth - 1)
        def _():
            at = F.at[b + 1, planes + 1, pl.ds(SUB, rows)]
            pltpu.make_async_copy(at, at, plane_recv.at[1, b]).wait()

        @pl.when(b >= early)
        def _():
            wait_mat(b)

        def rest(t, _):
            full(b, [2 * t, 2 * t + 1 + (tiles - 2) * (1 - late)])
            return 0

        lax.fori_loop(0, 1 + (tiles // 2 - 1) * late, rest, 0)

        def finish(t, _):
            ends(b, [1 + 3 * t + j for j in range(3)])
            return 0

        lax.fori_loop(0, (inner // 3) * (1 - late), finish, 0)

        @pl.when(b > 0)
        def _():
            shear(b - 1, recv, (1, b - 1), a2a_recv.at[1])

        return 0

    lax.fori_loop(0, blocks, block, 0)
    shear(last, final, (0, 0), a2a_recv.at[2])

    low = sub_id < part

    def compose(view, b, held):
        through = zero + 1.0
        total = [zero, zero]
        for k in range(n_depth):
            layer = order_s[view, k]
            one, two = [held[view, b, layer, pl.ds(h * SUB, SUB), :] for h in range(2)]
            total = [total[0] + through * one, total[1] + through * two]
            opacity = jnp.where(low, pltpu.roll(two, part, 0), two)
            through = through * (1.0 - opacity)
        return total

    def compose_last():
        through = zero + 1.0
        total = [zero, zero]
        for k in range(n_depth):
            layer = order_s[1, k]
            one, two = [final[0, 0, layer, pl.ds(h * SUB, SUB), :] for h in range(2)]
            total = [total[0] + through * one, total[1] + through * two]
            opacity = jnp.where(low, pltpu.roll(two, part, 0), two)
            through = through * (1.0 - opacity)
        return total

    def put(view, b, total):
        columns_b = pl.ds(pl.multiple_of(b * LANES, LANES), LANES)
        out_ref[view, pl.ds(0, SUB), columns_b] = total[0]
        out_ref[view, pl.ds(SUB, SUB), columns_b] = total[1]

    for view, count in ((1, last), (0, blocks)):
        at = recv.at[view, pl.ds(0, count), pl.ds(0, n_depth - 1)]
        pltpu.make_async_copy(at, at, a2a_recv.at[view]).wait()

    def some(b, _):
        for view in range(2):
            put(view, b, compose(view, b, recv))
        return 0

    lax.fori_loop(0, last, some, 0)
    put(0, last, compose(0, last, recv))

    at = final.at[0, 0, pl.ds(0, n_depth - 1)]
    pltpu.make_async_copy(at, at, a2a_recv.at[2]).wait()
    put(1, last, compose_last())

    for view in range(2):
        at = send.at[view, :, pl.ds(0, n_depth - 1)]
        pltpu.make_async_copy(at, at, a2a_send.at[view]).wait()

    @pl.when(area < n_area - 1)
    def _():
        for b in range(blocks):
            pltpu.make_async_copy(own.at[b], own.at[b], shear_send.at[b]).wait()
        pltpu.make_async_copy(edge_out.at[1], edge_out.at[1], edge_send.at[1]).wait()

    @pl.when(area > 0)
    def _():
        pltpu.make_async_copy(edge_out.at[0], edge_out.at[0], edge_send.at[0]).wait()

    @pl.when(depth < n_depth - 1)
    def _():
        at = F.at[pl.ds(1, blocks), 0, pl.ds(SUB, rows)]
        pltpu.make_async_copy(at, at, plane_send.at[0]).wait()

    @pl.when(depth > 0)
    def _():
        at = F.at[pl.ds(1, blocks), planes + 1, pl.ds(SUB, rows)]
        pltpu.make_async_copy(at, at, plane_send.at[1]).wait()


def solution(mesh):
    n_area, n_depth = mesh.shape["area"], mesh.shape["depth"]

    def shards(field, materials, tf_table, view_order, shear_offset):
        planes, rows, columns = field.shape
        blocks = columns // LANES
        part = rows // n_depth
        f32 = jnp.float32
        image = pl.pallas_call(
            functools.partial(kernel, n_area, n_depth),
            out_shape=jax.ShapeDtypeStruct((2, 4 * part, columns), f32),
            in_specs=[pl.BlockSpec(memory_space=pltpu.HBM)] * 5,
            out_specs=pl.BlockSpec(memory_space=pltpu.VMEM),
            scratch_shapes=[
                pltpu.VMEM((blocks + 2, planes + 2, rows + 2 * SUB, LANES), f32),
                pltpu.VMEM((blocks, planes, rows, LANES), jnp.int32),
                pltpu.SMEM(tf_table.shape, f32),
                pltpu.SMEM(view_order.shape, jnp.int32),
                pltpu.SMEM(shear_offset.shape, jnp.int32),
                pltpu.VMEM((2, blocks, planes, LANES), f32),
                pltpu.VMEM((2, blocks, planes, LANES), f32),
                pltpu.VMEM((blocks, 7, rows, LANES), f32),
                pltpu.VMEM((blocks, 4, rows, LANES), f32),
                pltpu.VMEM((blocks, 4, rows, LANES), f32),
                pltpu.VMEM((4, 2 * rows, LANES), f32),
                pltpu.VMEM((2, blocks, n_depth, 4 * part, LANES), f32),
                pltpu.VMEM((2, blocks, n_depth, 4 * part, LANES), f32),
                pltpu.VMEM((1, 1, n_depth, 4 * part, LANES), f32),
                pltpu.SemaphoreType.DMA((2 * blocks,)),
                pltpu.SemaphoreType.DMA((3,)),
                pltpu.SemaphoreType.DMA((2,)),
                pltpu.SemaphoreType.DMA((2, blocks)),
                pltpu.SemaphoreType.DMA((2,)),
                pltpu.SemaphoreType.DMA((2, blocks)),
                pltpu.SemaphoreType.DMA((blocks,)),
                pltpu.SemaphoreType.DMA((blocks,)),
                pltpu.SemaphoreType.DMA((2,)),
                pltpu.SemaphoreType.DMA((3,)),
            ],
            compiler_params=pltpu.CompilerParams(
                collective_id=0, has_side_effects=True, vmem_limit_bytes=60 * 2**20
            ),
            name="render",
        )(field, materials, tf_table, view_order, shear_offset)
        return image.reshape(2, 4, part, columns)

    in_specs = (P("depth", "area", None), P("depth", "area", None), P(), P(), P())
    out_specs = P(None, None, ("area", "depth"), None)
    return jax.shard_map(shards, mesh=mesh, in_specs=in_specs, out_specs=out_specs, check_vma=False)
```

```python
import functools

import jax
import jax.numpy as jnp
from jax import lax
from jax.experimental import pallas as pl
from jax.experimental.pallas import tpu as pltpu
from jax.sharding import PartitionSpec as P

MESH = pl.DeviceIdType.MESH
LANES = 128
SUB = 8
LIGHT = 0.7 * 0.24
EXP_SCALE = -0.25 * 1.4426950408889634


def gather(table, index, axis):
    dims = lax.GatherDimensionNumbers(
        offset_dims=(),
        collapsed_slice_dims=(axis,),
        start_index_map=(axis,),
        operand_batching_dims=(1 - axis,),
        start_indices_batching_dims=(1 - axis,),
    )
    return lax.gather(
        table, index[..., None], dims, (1, 1), mode=lax.GatherScatterMode.PROMISE_IN_BOUNDS
    )


def kernel(
    n_area,
    n_depth,
    field_hbm,
    mat_hbm,
    tf_hbm,
    order_hbm,
    shear_hbm,
    out_ref,
    F,
    M,
    tf_s,
    order_s,
    shear_s,
    edge_out,
    edge_in,
    state,
    own,
    near,
    window,
    send,
    recv,
    final,
    load_sem,
    small_sem,
    plane_send,
    plane_recv,
    edge_send,
    edge_recv,
    shear_send,
    shear_recv,
    a2a_send,
    a2a_recv,
):
    planes, rows, columns = field_hbm.shape
    blocks = columns // LANES
    tiles = rows // SUB
    part = rows // n_depth
    halves = SUB // part
    last = blocks - 1
    area, depth = lax.axis_index("area"), lax.axis_index("depth")
    zero = jnp.zeros((SUB, LANES), jnp.float32)

    def load_field(b):
        pltpu.make_async_copy(
            field_hbm.at[:, :, pl.ds(b * LANES, LANES)],
            F.at[b + 1, pl.ds(1, planes), pl.ds(SUB, rows)],
            load_sem.at[b],
        ).start()

    load_field(0)
    for b in range(blocks):
        if b + 1 < blocks:
            load_field(b + 1)
        pltpu.make_async_copy(
            mat_hbm.at[:, :, pl.ds(b * LANES, LANES)], M.at[b], load_sem.at[blocks + b]
        ).start()
    small = [
        pltpu.make_async_copy(src, dst, small_sem.at[i])
        for i, (src, dst) in enumerate(
            ((tf_hbm, tf_s), (order_hbm, order_s), (shear_hbm, shear_s))
        )
    ]
    for copy in small:
        copy.start()

    def wait_field(b):
        pltpu.make_async_copy(
            F.at[b + 1, pl.ds(1, planes), pl.ds(SUB, rows)],
            F.at[b + 1, pl.ds(1, planes), pl.ds(SUB, rows)],
            load_sem.at[b],
        ).wait()

    def wait_mat(b):
        pltpu.make_async_copy(M.at[b], M.at[b], load_sem.at[blocks + b]).wait()

    barrier = pltpu.get_barrier_semaphore()

    def greet(i, _):
        peer = lax.rem(depth + i, n_depth)
        pl.semaphore_signal(barrier, inc=1, device_id={"depth": peer}, device_id_type=MESH)
        return 0

    lax.fori_loop(1, n_depth, greet, 0)

    @pl.when(area > 0)
    def _():
        pl.semaphore_signal(barrier, inc=1, device_id={"area": area - 1}, device_id_type=MESH)

    @pl.when(area < n_area - 1)
    def _():
        pl.semaphore_signal(barrier, inc=1, device_id={"area": area + 1}, device_id_type=MESH)

    def clear(k, _):
        for r in range(tiles + 2):
            F[0, k, pl.ds(r * SUB, SUB), :] = zero
            F[blocks + 1, k, pl.ds(r * SUB, SUB), :] = zero
        return 0

    lax.fori_loop(0, planes + 2, clear, 0)

    def clear_plane(at):
        for b in range(blocks):
            for r in range(tiles):
                F[b + 1, at, pl.ds(SUB + r * SUB, SUB), :] = zero

    for side, outer in ((0, area == 0), (1, area == n_area - 1)):

        @pl.when(outer)
        def _():
            for b in range(blocks):
                edge_in[side, b] = jnp.zeros((planes, LANES), jnp.float32)

    @pl.when(depth == 0)
    def _():
        clear_plane(0)

    @pl.when(depth == n_depth - 1)
    def _():
        clear_plane(planes + 1)

    def pack_edges(b):
        for k in range(planes):
            edge_out[0, b, pl.ds(k, 1), :] = F[b + 1, k + 1, pl.ds(SUB, 1), :]
            edge_out[1, b, pl.ds(k, 1), :] = F[b + 1, k + 1, pl.ds(SUB + rows - 1, 1), :]

    for copy in small:
        copy.wait()
    sub_id = lax.broadcasted_iota(jnp.int32, (SUB, LANES), 0)
    lane_id = lax.broadcasted_iota(jnp.int32, (SUB, LANES), 1)
    is_first, is_last = lane_id == 0, lane_id == LANES - 1
    table = []
    for channel in range(3):
        pair = []
        for half in range(2):
            values = jnp.full((SUB, LANES), tf_s[channel, half * SUB], jnp.float32)
            for entry in range(1, SUB):
                values = jnp.where(sub_id == entry, tf_s[channel, half * SUB + entry], values)
            pair.append(values)
        table.append([LIGHT * values for values in pair])
    opacities = jnp.zeros((SUB, LANES), jnp.float32)
    for entry in range(tf_s.shape[1]):
        opacities = jnp.where(lane_id == entry, tf_s[3, entry], opacities)

    def cells(b, k, row):
        mid = pl.ds(pl.multiple_of(row + SUB, SUB), SUB)
        c = F[b + 1, k + 1, mid, :]
        gz = F[b + 1, k + 2, mid, :] - F[b + 1, k, mid, :]
        gy = F[b + 1, k + 1, pl.ds(row + SUB + 1, SUB), :] - F[b + 1, k + 1, pl.ds(row + SUB - 1, SUB), :]
        before = pltpu.roll(jnp.where(is_last, F[b, k + 1, mid, :], c), 1, 1)
        after = pltpu.roll(jnp.where(is_first, F[b + 2, k + 1, mid, :], c), LANES - 1, 1)
        gx = after - before
        gm2 = 0.25 * (gz * gz + gy * gy + gx * gx)
        lit = jnp.abs(gz + (0.3 / 0.24) * gy + (0.32 / 0.24) * gx)
        shade = 0.3 / LIGHT + lit * lax.rsqrt(gm2 + 1.0)
        m = M[b, k, pl.ds(pl.multiple_of(row, SUB), SUB), :]
        upper, index = m > SUB - 1, m & (SUB - 1)
        looked = [
            jnp.where(upper, gather(hi, index, 0), gather(lo, index, 0))
            for lo, hi in table
        ]
        a = gather(opacities, m, 1) * (1.0 - jnp.exp2(EXP_SCALE * (c * c + gm2)))
        return looked, shade * a, 1.0 - a

    def march(b, tile, first, last):
        row = tile * SUB
        through = zero + 1.0
        front, back = [zero] * 3, [zero] * 3
        for k in range(first, last):
            colour, sa, keep = cells(b, k, row)
            colour = [t * sa for t in colour]
            front = [f + c * through for f, c in zip(front, colour)]
            back = [f * keep + c for f, c in zip(back, colour)]
            through = through * keep
        return through, front, back

    def interior(b, several):
        marched = [march(b, tile, 1, planes - 1) for tile in several]
        for tile, (through, front, back) in zip(several, marched):
            at = pl.ds(pl.multiple_of(tile * SUB, SUB), SUB)
            for i, value in enumerate([through, *front, *back]):
                state[b, i, at, :] = value

    def keep(b, tile, front, back, through):
        at = pl.ds(pl.multiple_of(tile * SUB, SUB), SUB)
        opacity = 1.0 - through
        for i, (first, second) in enumerate(zip([*front, opacity], [*back, opacity])):
            own[b, i, at, :] = second
            for half in range(halves):
                send[0, b, tile * halves + half, pl.ds(i * part, part), :] = first[
                    half * part : (half + 1) * part
                ]

    def leave(b, tile):
        at = pl.ds(pl.multiple_of(tile * SUB, SUB), SUB)

        @pl.when(area < n_area - 1)
        def _():
            pltpu.make_async_remote_copy(
                src_ref=own.at[b, :, at],
                dst_ref=near.at[b, :, at],
                send_sem=shear_send.at[b],
                recv_sem=shear_recv.at[b],
                device_id={"area": area + 1},
                device_id_type=MESH,
            ).start()

        for half in range(halves):
            peer = tile * halves + half

            @pl.when(peer != depth)
            def _():
                part_copy(0, b, peer).start()

            @pl.when(peer == depth)
            def _():
                recv[0, b, depth] = send[0, b, depth]

    def full(b, several):
        marched = [march(b, tile, 0, planes) for tile in several]
        for tile, (through, front, back) in zip(several, marched):
            keep(b, tile, front, back, through)
        for tile in several:
            leave(b, tile)

    def ends(b, several):
        for tile in several:
            row = tile * SUB
            at = pl.ds(pl.multiple_of(row, SUB), SUB)
            colour0, sa0, keep0 = cells(b, 0, row)
            colour1, sa1, keep1 = cells(b, planes - 1, row)
            through = state[b, 0, at, :]
            front, back = [], []
            for i in range(3):
                c0, c1 = colour0[i] * sa0, colour1[i] * sa1
                front.append(c0 + keep0 * (state[b, 1 + i, at, :] + through * c1))
                back.append(c1 + keep1 * (state[b, 4 + i, at, :] + through * c0))
            keep(b, tile, front, back, through * keep0 * keep1)
        for tile in several:
            leave(b, tile)

    def part_copy(view, b, peer):
        return pltpu.make_async_remote_copy(
            src_ref=send.at[view, b, peer],
            dst_ref=recv.at[view, b, depth],
            send_sem=a2a_send.at[view],
            recv_sem=a2a_recv.at[view],
            device_id={"depth": peer},
            device_id_type=MESH,
        )

    offset = shear_s[depth]

    edge = int(n_depth**0.5)
    far = sorted(
        ((x, z) for x in range(edge) for z in range(edge) if x or z),
        key=lambda p: -min(p[0], edge - p[0]) - min(p[1], edge - p[1]),
    )

    def peer_at(x, z):
        return lax.rem(depth // edge + x, edge) * edge + lax.rem(depth + z, edge)

    def shear(b, place, slot, sems):
        @pl.when(area > 0)
        def _():
            pltpu.make_async_copy(near.at[b], near.at[b], shear_recv.at[b]).wait()
            for i in range(4):
                window[i, pl.ds(0, rows), :] = near[b, i]

        for i in range(4):
            window[i, pl.ds(rows, rows), :] = own[b, i]
        for tile in range(tiles):
            for i in range(4):
                moved = window[i, pl.ds(rows + tile * SUB - offset, SUB), :]
                for half in range(halves):
                    send[1, b, tile * halves + half, pl.ds(i * part, part), :] = moved[
                        half * part : (half + 1) * part
                    ]

        for x, z in far:
            peer = peer_at(x, z)
            pltpu.make_async_remote_copy(
                src_ref=send.at[1, b, peer],
                dst_ref=place.at[slot[0], slot[1], depth],
                send_sem=a2a_send.at[1],
                recv_sem=sems,
                device_id={"depth": peer},
                device_id_type=MESH,
            ).start()
        place[slot[0], slot[1], depth] = send[1, b, depth]

    inner = tiles - 2
    early = 2

    def plane_copy(b, src, dst, way, peer):
        return pltpu.make_async_remote_copy(
            src_ref=F.at[b + 1, src + 1, pl.ds(SUB, rows)],
            dst_ref=F.at[b + 1, dst, pl.ds(SUB, rows)],
            send_sem=plane_send.at[way],
            recv_sem=plane_recv.at[way, b],
            device_id={"depth": peer},
            device_id_type=MESH,
        )

    def send_planes(b):
        @pl.when(depth < n_depth - 1)
        def _():
            plane_copy(b, planes - 1, 0, 0, depth + 1).start()

        @pl.when(depth > 0)
        def _():
            plane_copy(b, 0, planes + 1, 1, depth - 1).start()

    def edge_copy(b, side, peer):
        return pltpu.make_async_remote_copy(
            src_ref=edge_out.at[side, b],
            dst_ref=edge_in.at[1 - side, b],
            send_sem=edge_send.at[side],
            recv_sem=edge_recv.at[1 - side, b],
            device_id={"area": peer},
            device_id_type=MESH,
        )

    def send_edges(b):
        pack_edges(b)

        @pl.when(area < n_area - 1)
        def _():
            edge_copy(b, 1, area + 1).start()

        @pl.when(area > 0)
        def _():
            edge_copy(b, 0, area - 1).start()

    def early_tile(i, _):
        b = i // (inner // 3)
        tile = 1 + 3 * (i % (inner // 3))

        @pl.when(tile == 1)
        def _():
            wait_mat(b)

        interior(b, [tile + j for j in range(3)])
        return 0

    def early_tile_and_halo(i, _):
        for b in range(1, blocks):

            @pl.when(i == b - 1)
            def _():
                if b > 1:
                    wait_field(b)
                send_planes(b)
                send_edges(b)

        return early_tile(i, 0)

    @pl.when(jnp.logical_and(area > 0, area < n_area - 1))
    def _():
        pl.semaphore_wait(barrier, n_depth - 1 + 2)

    @pl.when(jnp.logical_or(area == 0, area == n_area - 1))
    def _():
        pl.semaphore_wait(barrier, n_depth - 1 + 1)

    wait_field(0)
    send_planes(0)
    wait_field(1)
    send_edges(0)

    @pl.when(area == 0)
    def _():
        for i in range(4):
            for tile in range(tiles):
                window[i, pl.ds(tile * SUB, SUB), :] = zero

    lax.fori_loop(0, (inner // 3) * early, early_tile_and_halo, 0)

    def block(b, _):
        late = jnp.where(b >= early, 1, 0)

        for side, outer, at_row in ((0, area == 0, SUB - 1), (1, area == n_area - 1, SUB + rows)):

            @pl.when(jnp.logical_not(outer))
            def _():
                at = edge_in.at[side, b]
                pltpu.make_async_copy(at, at, edge_recv.at[side, b]).wait()

            for k in range(planes):
                value = edge_in[side, b, pl.ds(k, 1), :]
                F[b + 1, k + 1, pl.ds(at_row, 1), :] = value

        @pl.when(depth > 0)
        def _():
            at = F.at[b + 1, 0, pl.ds(SUB, rows)]
            pltpu.make_async_copy(at, at, plane_recv.at[0, b]).wait()

        @pl.when(depth < n_depth - 1)
        def _():
            at = F.at[b + 1, planes + 1, pl.ds(SUB, rows)]
            pltpu.make_async_copy(at, at, plane_recv.at[1, b]).wait()

        @pl.when(b >= early)
        def _():
            wait_mat(b)

        def rest(t, _):
            full(b, [2 * t, 2 * t + 1 + (tiles - 2) * (1 - late)])

            @pl.when(jnp.logical_and(b == early, t == 1))
            def _():
                shear(0, recv, (1, 0), a2a_recv.at[1])

            return 0

        lax.fori_loop(0, 1 + (tiles // 2 - 1) * late, rest, 0)

        def finish(t, _):
            ends(b, [1 + t + j for j in range(inner)])
            return 0

        lax.fori_loop(0, 1 - late, finish, 0)

        @pl.when(b >= early)
        def _():
            shear(b - 1, recv, (1, b - 1), a2a_recv.at[1])

        return 0

    lax.fori_loop(0, blocks, block, 0)
    shear(last, final, (0, 0), a2a_recv.at[2])

    low = sub_id < part

    def compose(view, b, held):
        through = zero + 1.0
        total = [zero, zero]
        for k in range(n_depth):
            layer = order_s[view, k]
            one, two = [held[view, b, layer, pl.ds(h * SUB, SUB), :] for h in range(2)]
            total = [total[0] + through * one, total[1] + through * two]
            opacity = jnp.where(low, pltpu.roll(two, part, 0), two)
            through = through * (1.0 - opacity)
        return total

    def compose_last():
        through = zero + 1.0
        total = [zero, zero]
        for k in range(n_depth):
            layer = order_s[1, k]
            one, two = [final[0, 0, layer, pl.ds(h * SUB, SUB), :] for h in range(2)]
            total = [total[0] + through * one, total[1] + through * two]
            opacity = jnp.where(low, pltpu.roll(two, part, 0), two)
            through = through * (1.0 - opacity)
        return total

    def put(view, b, total):
        columns_b = pl.ds(pl.multiple_of(b * LANES, LANES), LANES)
        out_ref[view, pl.ds(0, SUB), columns_b] = total[0]
        out_ref[view, pl.ds(SUB, SUB), columns_b] = total[1]

    for view, count in ((1, last), (0, blocks)):
        at = recv.at[view, pl.ds(0, count), pl.ds(0, n_depth - 1)]
        pltpu.make_async_copy(at, at, a2a_recv.at[view]).wait()

    def some(b, _):
        for view in range(2):
            put(view, b, compose(view, b, recv))
        return 0

    lax.fori_loop(0, last, some, 0)
    put(0, last, compose(0, last, recv))

    at = final.at[0, 0, pl.ds(0, n_depth - 1)]
    pltpu.make_async_copy(at, at, a2a_recv.at[2]).wait()
    put(1, last, compose_last())

    for view in range(2):
        at = send.at[view, :, pl.ds(0, n_depth - 1)]
        pltpu.make_async_copy(at, at, a2a_send.at[view]).wait()

    @pl.when(area < n_area - 1)
    def _():
        for b in range(blocks):
            pltpu.make_async_copy(own.at[b], own.at[b], shear_send.at[b]).wait()
        pltpu.make_async_copy(edge_out.at[1], edge_out.at[1], edge_send.at[1]).wait()

    @pl.when(area > 0)
    def _():
        pltpu.make_async_copy(edge_out.at[0], edge_out.at[0], edge_send.at[0]).wait()

    @pl.when(depth < n_depth - 1)
    def _():
        at = F.at[pl.ds(1, blocks), 0, pl.ds(SUB, rows)]
        pltpu.make_async_copy(at, at, plane_send.at[0]).wait()

    @pl.when(depth > 0)
    def _():
        at = F.at[pl.ds(1, blocks), planes + 1, pl.ds(SUB, rows)]
        pltpu.make_async_copy(at, at, plane_send.at[1]).wait()


def solution(mesh):
    n_area, n_depth = mesh.shape["area"], mesh.shape["depth"]

    def shards(field, materials, tf_table, view_order, shear_offset):
        planes, rows, columns = field.shape
        blocks = columns // LANES
        part = rows // n_depth
        f32 = jnp.float32
        image = pl.pallas_call(
            functools.partial(kernel, n_area, n_depth),
            out_shape=jax.ShapeDtypeStruct((2, 4 * part, columns), f32),
            in_specs=[pl.BlockSpec(memory_space=pltpu.HBM)] * 5,
            out_specs=pl.BlockSpec(memory_space=pltpu.VMEM),
            scratch_shapes=[
                pltpu.VMEM((blocks + 2, planes + 2, rows + 2 * SUB, LANES), f32),
                pltpu.VMEM((blocks, planes, rows, LANES), jnp.int32),
                pltpu.SMEM(tf_table.shape, f32),
                pltpu.SMEM(view_order.shape, jnp.int32),
                pltpu.SMEM(shear_offset.shape, jnp.int32),
                pltpu.VMEM((2, blocks, planes, LANES), f32),
                pltpu.VMEM((2, blocks, planes, LANES), f32),
                pltpu.VMEM((blocks, 7, rows, LANES), f32),
                pltpu.VMEM((blocks, 4, rows, LANES), f32),
                pltpu.VMEM((blocks, 4, rows, LANES), f32),
                pltpu.VMEM((4, 2 * rows, LANES), f32),
                pltpu.VMEM((2, blocks, n_depth, 4 * part, LANES), f32),
                pltpu.VMEM((2, blocks, n_depth, 4 * part, LANES), f32),
                pltpu.VMEM((1, 1, n_depth, 4 * part, LANES), f32),
                pltpu.SemaphoreType.DMA((2 * blocks,)),
                pltpu.SemaphoreType.DMA((3,)),
                pltpu.SemaphoreType.DMA((2,)),
                pltpu.SemaphoreType.DMA((2, blocks)),
                pltpu.SemaphoreType.DMA((2,)),
                pltpu.SemaphoreType.DMA((2, blocks)),
                pltpu.SemaphoreType.DMA((blocks,)),
                pltpu.SemaphoreType.DMA((blocks,)),
                pltpu.SemaphoreType.DMA((2,)),
                pltpu.SemaphoreType.DMA((3,)),
            ],
            compiler_params=pltpu.CompilerParams(
                collective_id=0, has_side_effects=True, vmem_limit_bytes=60 * 2**20
            ),
            name="render",
        )(field, materials, tf_table, view_order, shear_offset)
        return image.reshape(2, 4, part, columns)

    in_specs = (P("depth", "area", None), P("depth", "area", None), P(), P(), P())
    out_specs = P(None, None, ("area", "depth"), None)
    return jax.shard_map(shards, mesh=mesh, in_specs=in_specs, out_specs=out_specs, check_vma=False)
```

```python
import functools

import jax
import jax.numpy as jnp
from jax import lax
from jax.experimental import pallas as pl
from jax.experimental.pallas import tpu as pltpu
from jax.sharding import PartitionSpec as P

MESH = pl.DeviceIdType.MESH
LANES = 128
SUB = 8
LIGHT = 0.7 * 0.24
EXP_SCALE = -0.25 * 1.4426950408889634


def gather(table, index, axis):
    dims = lax.GatherDimensionNumbers(
        offset_dims=(),
        collapsed_slice_dims=(axis,),
        start_index_map=(axis,),
        operand_batching_dims=(1 - axis,),
        start_indices_batching_dims=(1 - axis,),
    )
    return lax.gather(
        table, index[..., None], dims, (1, 1), mode=lax.GatherScatterMode.PROMISE_IN_BOUNDS
    )


def kernel(
    n_area,
    n_depth,
    field_hbm,
    mat_hbm,
    tf_hbm,
    order_hbm,
    shear_hbm,
    out_ref,
    F,
    M,
    tf_s,
    order_s,
    shear_s,
    edge_out,
    edge_in,
    state,
    own,
    near,
    window,
    send,
    recv,
    final,
    load_sem,
    small_sem,
    plane_send,
    plane_recv,
    edge_send,
    edge_recv,
    shear_send,
    shear_recv,
    a2a_send,
    a2a_recv,
):
    planes, rows, columns = field_hbm.shape
    blocks = columns // LANES
    tiles = rows // SUB
    part = rows // n_depth
    halves = SUB // part
    last = blocks - 1
    area, depth = lax.axis_index("area"), lax.axis_index("depth")
    zero = jnp.zeros((SUB, LANES), jnp.float32)

    def load_field(b):
        pltpu.make_async_copy(
            field_hbm.at[:, :, pl.ds(b * LANES, LANES)],
            F.at[b + 1, pl.ds(1, planes), pl.ds(SUB, rows)],
            load_sem.at[b],
        ).start()

    load_field(0)
    for b in range(blocks):
        if b + 1 < blocks:
            load_field(b + 1)
        pltpu.make_async_copy(
            mat_hbm.at[:, :, pl.ds(b * LANES, LANES)], M.at[b], load_sem.at[blocks + b]
        ).start()
    small = [
        pltpu.make_async_copy(src, dst, small_sem.at[i])
        for i, (src, dst) in enumerate(
            ((tf_hbm, tf_s), (order_hbm, order_s), (shear_hbm, shear_s))
        )
    ]
    for copy in small:
        copy.start()

    def wait_field(b):
        pltpu.make_async_copy(
            F.at[b + 1, pl.ds(1, planes), pl.ds(SUB, rows)],
            F.at[b + 1, pl.ds(1, planes), pl.ds(SUB, rows)],
            load_sem.at[b],
        ).wait()

    def wait_mat(b):
        pltpu.make_async_copy(M.at[b], M.at[b], load_sem.at[blocks + b]).wait()

    barrier = pltpu.get_barrier_semaphore()

    def greet(i, _):
        peer = lax.rem(depth + i, n_depth)
        pl.semaphore_signal(barrier, inc=1, device_id={"depth": peer}, device_id_type=MESH)
        return 0

    lax.fori_loop(1, n_depth, greet, 0)

    @pl.when(area > 0)
    def _():
        pl.semaphore_signal(barrier, inc=1, device_id={"area": area - 1}, device_id_type=MESH)

    @pl.when(area < n_area - 1)
    def _():
        pl.semaphore_signal(barrier, inc=1, device_id={"area": area + 1}, device_id_type=MESH)

    def clear(k, _):
        for r in range(tiles + 2):
            F[0, k, pl.ds(r * SUB, SUB), :] = zero
            F[blocks + 1, k, pl.ds(r * SUB, SUB), :] = zero
        return 0

    lax.fori_loop(0, planes + 2, clear, 0)

    def clear_plane(at):
        for b in range(blocks):
            for r in range(tiles):
                F[b + 1, at, pl.ds(SUB + r * SUB, SUB), :] = zero

    for side, outer in ((0, area == 0), (1, area == n_area - 1)):

        @pl.when(outer)
        def _():
            for b in range(blocks):
                edge_in[side, b] = jnp.zeros((planes, LANES), jnp.float32)

    @pl.when(depth == 0)
    def _():
        clear_plane(0)

    @pl.when(depth == n_depth - 1)
    def _():
        clear_plane(planes + 1)

    def pack_edges(b):
        for k in range(planes):
            edge_out[0, b, pl.ds(k, 1), :] = F[b + 1, k + 1, pl.ds(SUB, 1), :]
            edge_out[1, b, pl.ds(k, 1), :] = F[b + 1, k + 1, pl.ds(SUB + rows - 1, 1), :]

    for copy in small:
        copy.wait()
    sub_id = lax.broadcasted_iota(jnp.int32, (SUB, LANES), 0)
    lane_id = lax.broadcasted_iota(jnp.int32, (SUB, LANES), 1)
    is_first, is_last = lane_id == 0, lane_id == LANES - 1
    table = []
    for channel in range(3):
        pair = []
        for half in range(2):
            values = jnp.full((SUB, LANES), tf_s[channel, half * SUB], jnp.float32)
            for entry in range(1, SUB):
                values = jnp.where(sub_id == entry, tf_s[channel, half * SUB + entry], values)
            pair.append(values)
        table.append([LIGHT * values for values in pair])
    opacities = jnp.zeros((SUB, LANES), jnp.float32)
    for entry in range(tf_s.shape[1]):
        opacities = jnp.where(lane_id == entry, tf_s[3, entry], opacities)

    def cells(b, k, row):
        mid = pl.ds(pl.multiple_of(row + SUB, SUB), SUB)
        c = F[b + 1, k + 1, mid, :]
        gz = F[b + 1, k + 2, mid, :] - F[b + 1, k, mid, :]
        gy = F[b + 1, k + 1, pl.ds(row + SUB + 1, SUB), :] - F[b + 1, k + 1, pl.ds(row + SUB - 1, SUB), :]
        before = pltpu.roll(jnp.where(is_last, F[b, k + 1, mid, :], c), 1, 1)
        after = pltpu.roll(jnp.where(is_first, F[b + 2, k + 1, mid, :], c), LANES - 1, 1)
        gx = after - before
        gm2 = 0.25 * (gz * gz + gy * gy + gx * gx)
        lit = jnp.abs(gz + (0.3 / 0.24) * gy + (0.32 / 0.24) * gx)
        shade = 0.3 / LIGHT + lit * lax.rsqrt(gm2 + 1.0)
        m = M[b, k, pl.ds(pl.multiple_of(row, SUB), SUB), :]
        upper, index = m > SUB - 1, m & (SUB - 1)
        looked = [
            jnp.where(upper, gather(hi, index, 0), gather(lo, index, 0))
            for lo, hi in table
        ]
        a = gather(opacities, m, 1) * (1.0 - jnp.exp2(EXP_SCALE * (c * c + gm2)))
        return looked, shade * a, 1.0 - a

    def march(b, tile, first, last):
        row = tile * SUB
        through = zero + 1.0
        front, back = [zero] * 3, [zero] * 3
        for k in range(first, last):
            colour, sa, keep = cells(b, k, row)
            colour = [t * sa for t in colour]
            front = [f + c * through for f, c in zip(front, colour)]
            back = [f * keep + c for f, c in zip(back, colour)]
            through = through * keep
        return through, front, back

    def interior(b, several):
        marched = [march(b, tile, 1, planes - 1) for tile in several]
        for tile, (through, front, back) in zip(several, marched):
            at = pl.ds(pl.multiple_of(tile * SUB, SUB), SUB)
            for i, value in enumerate([through, *front, *back]):
                state[b, i, at, :] = value

    def keep(b, tile, front, back, through):
        at = pl.ds(pl.multiple_of(tile * SUB, SUB), SUB)
        opacity = 1.0 - through
        for i, (first, second) in enumerate(zip([*front, opacity], [*back, opacity])):
            own[b, i, at, :] = second
            for half in range(halves):
                send[0, b, tile * halves + half, pl.ds(i * part, part), :] = first[
                    half * part : (half + 1) * part
                ]

    def leave(b, tile):
        at = pl.ds(pl.multiple_of(tile * SUB, SUB), SUB)

        @pl.when(area < n_area - 1)
        def _():
            pltpu.make_async_remote_copy(
                src_ref=own.at[b, :, at],
                dst_ref=near.at[b, :, at],
                send_sem=shear_send.at[b],
                recv_sem=shear_recv.at[b],
                device_id={"area": area + 1},
                device_id_type=MESH,
            ).start()

        for half in range(halves):
            peer = tile * halves + half

            @pl.when(peer != depth)
            def _():
                part_copy(0, b, peer).start()

            @pl.when(peer == depth)
            def _():
                recv[0, b, depth] = send[0, b, depth]

    def full(b, several):
        marched = [march(b, tile, 0, planes) for tile in several]
        for tile, (through, front, back) in zip(several, marched):
            keep(b, tile, front, back, through)
        for tile in several:
            leave(b, tile)

    def ends(b, several):
        for tile in several:
            row = tile * SUB
            at = pl.ds(pl.multiple_of(row, SUB), SUB)
            colour0, sa0, keep0 = cells(b, 0, row)
            colour1, sa1, keep1 = cells(b, planes - 1, row)
            through = state[b, 0, at, :]
            front, back = [], []
            for i in range(3):
                c0, c1 = colour0[i] * sa0, colour1[i] * sa1
                front.append(c0 + keep0 * (state[b, 1 + i, at, :] + through * c1))
                back.append(c1 + keep1 * (state[b, 4 + i, at, :] + through * c0))
            keep(b, tile, front, back, through * keep0 * keep1)
        for tile in several:
            leave(b, tile)

    def part_copy(view, b, peer):
        return pltpu.make_async_remote_copy(
            src_ref=send.at[view, b, peer],
            dst_ref=recv.at[view, b, depth],
            send_sem=a2a_send.at[view],
            recv_sem=a2a_recv.at[view],
            device_id={"depth": peer},
            device_id_type=MESH,
        )

    offset = shear_s[depth]

    edge = int(n_depth**0.5)
    far = sorted(
        ((x, z) for x in range(edge) for z in range(edge) if x or z),
        key=lambda p: -min(p[0], edge - p[0]) - min(p[1], edge - p[1]),
    )

    def peer_at(x, z):
        return lax.rem(depth // edge + x, edge) * edge + lax.rem(depth + z, edge)

    def shear(b, place, slot, sems):
        @pl.when(area > 0)
        def _():
            pltpu.make_async_copy(near.at[b], near.at[b], shear_recv.at[b]).wait()
            for i in range(4):
                window[i, pl.ds(0, rows), :] = near[b, i]

        for i in range(4):
            window[i, pl.ds(rows, rows), :] = own[b, i]
        for tile in range(tiles):
            for i in range(4):
                moved = window[i, pl.ds(rows + tile * SUB - offset, SUB), :]
                for half in range(halves):
                    send[1, b, tile * halves + half, pl.ds(i * part, part), :] = moved[
                        half * part : (half + 1) * part
                    ]

        for x, z in far:
            peer = peer_at(x, z)
            pltpu.make_async_remote_copy(
                src_ref=send.at[1, b, peer],
                dst_ref=place.at[slot[0], slot[1], depth],
                send_sem=a2a_send.at[1],
                recv_sem=sems,
                device_id={"depth": peer},
                device_id_type=MESH,
            ).start()
        place[slot[0], slot[1], depth] = send[1, b, depth]

    inner = tiles - 2
    early = 2

    def plane_copy(b, src, dst, way, peer):
        return pltpu.make_async_remote_copy(
            src_ref=F.at[b + 1, src + 1, pl.ds(SUB, rows)],
            dst_ref=F.at[b + 1, dst, pl.ds(SUB, rows)],
            send_sem=plane_send.at[way],
            recv_sem=plane_recv.at[way, b],
            device_id={"depth": peer},
            device_id_type=MESH,
        )

    def send_planes(b):
        @pl.when(depth < n_depth - 1)
        def _():
            plane_copy(b, planes - 1, 0, 0, depth + 1).start()

        @pl.when(depth > 0)
        def _():
            plane_copy(b, 0, planes + 1, 1, depth - 1).start()

    def edge_copy(b, side, peer):
        return pltpu.make_async_remote_copy(
            src_ref=edge_out.at[side, b],
            dst_ref=edge_in.at[1 - side, b],
            send_sem=edge_send.at[side],
            recv_sem=edge_recv.at[1 - side, b],
            device_id={"area": peer},
            device_id_type=MESH,
        )

    def send_edges(b):
        pack_edges(b)

        @pl.when(area < n_area - 1)
        def _():
            edge_copy(b, 1, area + 1).start()

        @pl.when(area > 0)
        def _():
            edge_copy(b, 0, area - 1).start()

    def early_tile(i, _):
        b = i // (inner // 3)
        tile = 1 + 3 * (i % (inner // 3))

        @pl.when(tile == 1)
        def _():
            wait_mat(b)

        interior(b, [tile + j for j in range(3)])
        return 0

    def early_tile_and_halo(i, _):
        for b in range(1, blocks):

            @pl.when(i == b)
            def _():
                if b > 1:
                    wait_field(b)
                send_planes(b)
                send_edges(b)

        return early_tile(i, 0)

    @pl.when(jnp.logical_and(area > 0, area < n_area - 1))
    def _():
        pl.semaphore_wait(barrier, n_depth - 1 + 2)

    @pl.when(jnp.logical_or(area == 0, area == n_area - 1))
    def _():
        pl.semaphore_wait(barrier, n_depth - 1 + 1)

    wait_field(0)
    send_planes(0)
    wait_field(1)
    send_edges(0)

    @pl.when(area == 0)
    def _():
        for i in range(4):
            for tile in range(tiles):
                window[i, pl.ds(tile * SUB, SUB), :] = zero

    lax.fori_loop(0, (inner // 3) * early, early_tile_and_halo, 0)

    def block(b, _):
        late = jnp.where(b >= early, 1, 0)

        for side, outer, at_row in ((0, area == 0, SUB - 1), (1, area == n_area - 1, SUB + rows)):

            @pl.when(jnp.logical_not(outer))
            def _():
                at = edge_in.at[side, b]
                pltpu.make_async_copy(at, at, edge_recv.at[side, b]).wait()

            for k in range(planes):
                value = edge_in[side, b, pl.ds(k, 1), :]
                F[b + 1, k + 1, pl.ds(at_row, 1), :] = value

        @pl.when(depth > 0)
        def _():
            at = F.at[b + 1, 0, pl.ds(SUB, rows)]
            pltpu.make_async_copy(at, at, plane_recv.at[0, b]).wait()

        @pl.when(depth < n_depth - 1)
        def _():
            at = F.at[b + 1, planes + 1, pl.ds(SUB, rows)]
            pltpu.make_async_copy(at, at, plane_recv.at[1, b]).wait()

        @pl.when(b >= early)
        def _():
            wait_mat(b)

        @pl.when(late == 0)
        def _():
            full(b, [0, tiles - 1])

        def rest(t, _):
            full(b, [4 * t + j for j in range(4)])

            @pl.when(jnp.logical_and(b == early, t == 0))
            def _():
                shear(0, recv, (1, 0), a2a_recv.at[1])

            return 0

        lax.fori_loop(0, (tiles // 4) * late, rest, 0)

        def finish(t, _):
            ends(b, [1 + t + j for j in range(inner)])
            return 0

        lax.fori_loop(0, 1 - late, finish, 0)

        @pl.when(b >= early)
        def _():
            shear(b - 1, recv, (1, b - 1), a2a_recv.at[1])

        return 0

    lax.fori_loop(0, blocks, block, 0)
    shear(last, final, (0, 0), a2a_recv.at[2])

    low = sub_id < part

    def compose(view, b, held):
        through = zero + 1.0
        total = [zero, zero]
        for k in range(n_depth):
            layer = order_s[view, k]
            one, two = [held[view, b, layer, pl.ds(h * SUB, SUB), :] for h in range(2)]
            total = [total[0] + through * one, total[1] + through * two]
            opacity = jnp.where(low, pltpu.roll(two, part, 0), two)
            through = through * (1.0 - opacity)
        return total

    def compose_last():
        through = zero + 1.0
        total = [zero, zero]
        for k in range(n_depth):
            layer = order_s[1, k]
            one, two = [final[0, 0, layer, pl.ds(h * SUB, SUB), :] for h in range(2)]
            total = [total[0] + through * one, total[1] + through * two]
            opacity = jnp.where(low, pltpu.roll(two, part, 0), two)
            through = through * (1.0 - opacity)
        return total

    def put(view, b, total):
        columns_b = pl.ds(pl.multiple_of(b * LANES, LANES), LANES)
        out_ref[view, pl.ds(0, SUB), columns_b] = total[0]
        out_ref[view, pl.ds(SUB, SUB), columns_b] = total[1]

    for view, count in ((1, last), (0, blocks)):
        at = recv.at[view, pl.ds(0, count), pl.ds(0, n_depth - 1)]
        pltpu.make_async_copy(at, at, a2a_recv.at[view]).wait()

    def some(b, _):
        for view in range(2):
            put(view, b, compose(view, b, recv))
        return 0

    lax.fori_loop(0, last, some, 0)
    put(0, last, compose(0, last, recv))

    at = final.at[0, 0, pl.ds(0, n_depth - 1)]
    pltpu.make_async_copy(at, at, a2a_recv.at[2]).wait()
    put(1, last, compose_last())

    for view in range(2):
        at = send.at[view, :, pl.ds(0, n_depth - 1)]
        pltpu.make_async_copy(at, at, a2a_send.at[view]).wait()

    @pl.when(area < n_area - 1)
    def _():
        for b in range(blocks):
            pltpu.make_async_copy(own.at[b], own.at[b], shear_send.at[b]).wait()
        pltpu.make_async_copy(edge_out.at[1], edge_out.at[1], edge_send.at[1]).wait()

    @pl.when(area > 0)
    def _():
        pltpu.make_async_copy(edge_out.at[0], edge_out.at[0], edge_send.at[0]).wait()

    @pl.when(depth < n_depth - 1)
    def _():
        at = F.at[pl.ds(1, blocks), 0, pl.ds(SUB, rows)]
        pltpu.make_async_copy(at, at, plane_send.at[0]).wait()

    @pl.when(depth > 0)
    def _():
        at = F.at[pl.ds(1, blocks), planes + 1, pl.ds(SUB, rows)]
        pltpu.make_async_copy(at, at, plane_send.at[1]).wait()


def solution(mesh):
    n_area, n_depth = mesh.shape["area"], mesh.shape["depth"]

    def shards(field, materials, tf_table, view_order, shear_offset):
        planes, rows, columns = field.shape
        blocks = columns // LANES
        part = rows // n_depth
        f32 = jnp.float32
        image = pl.pallas_call(
            functools.partial(kernel, n_area, n_depth),
            out_shape=jax.ShapeDtypeStruct((2, 4 * part, columns), f32),
            in_specs=[pl.BlockSpec(memory_space=pltpu.HBM)] * 5,
            out_specs=pl.BlockSpec(memory_space=pltpu.VMEM),
            scratch_shapes=[
                pltpu.VMEM((blocks + 2, planes + 2, rows + 2 * SUB, LANES), f32),
                pltpu.VMEM((blocks, planes, rows, LANES), jnp.int32),
                pltpu.SMEM(tf_table.shape, f32),
                pltpu.SMEM(view_order.shape, jnp.int32),
                pltpu.SMEM(shear_offset.shape, jnp.int32),
                pltpu.VMEM((2, blocks, planes, LANES), f32),
                pltpu.VMEM((2, blocks, planes, LANES), f32),
                pltpu.VMEM((blocks, 7, rows, LANES), f32),
                pltpu.VMEM((blocks, 4, rows, LANES), f32),
                pltpu.VMEM((blocks, 4, rows, LANES), f32),
                pltpu.VMEM((4, 2 * rows, LANES), f32),
                pltpu.VMEM((2, blocks, n_depth, 4 * part, LANES), f32),
                pltpu.VMEM((2, blocks, n_depth, 4 * part, LANES), f32),
                pltpu.VMEM((1, 1, n_depth, 4 * part, LANES), f32),
                pltpu.SemaphoreType.DMA((2 * blocks,)),
                pltpu.SemaphoreType.DMA((3,)),
                pltpu.SemaphoreType.DMA((2,)),
                pltpu.SemaphoreType.DMA((2, blocks)),
                pltpu.SemaphoreType.DMA((2,)),
                pltpu.SemaphoreType.DMA((2, blocks)),
                pltpu.SemaphoreType.DMA((blocks,)),
                pltpu.SemaphoreType.DMA((blocks,)),
                pltpu.SemaphoreType.DMA((2,)),
                pltpu.SemaphoreType.DMA((3,)),
            ],
            compiler_params=pltpu.CompilerParams(
                collective_id=0, has_side_effects=True, vmem_limit_bytes=60 * 2**20
            ),
            name="render",
        )(field, materials, tf_table, view_order, shear_offset)
        return image.reshape(2, 4, part, columns)

    in_specs = (P("depth", "area", None), P("depth", "area", None), P(), P(), P())
    out_specs = P(None, None, ("area", "depth"), None)
    return jax.shard_map(shards, mesh=mesh, in_specs=in_specs, out_specs=out_specs, check_vma=False)
```
